32 devices in a mesh: section: 2 (over y), dp: 4 (over x, core), expert: 4 (over z).
Axes of the slice: x: 2, y: 2, z: 4, core: 2. Of those that a mesh axis runs over, the one named last changes fastest.
Arguments:
- activations: bfloat16 [2, 256, 4096], P('section', 'expert'), may hold values from -6 to 6
- routes: int32 [2, 256, 8], P('section', 'expert'), may hold values from 0 to 31, all different within a row; in each aligned block of 64 rows (0 to 63, 64 to 127, ..., all dimensions but the last counted through in order) at most 16 rows name the same one
- gate_weights: float32 [2, 256, 8], P('section', 'expert'), may hold values from 0.05 to 0.5
- norm_gain: bfloat16 [4096], replicated, may hold values from 0.099609375 to 1.8984375
- gate_up_weights: bfloat16 [32, 2, 1536, 4096], P('expert', None, 'dp'), may hold values from -0.09375 to 0.09375
- down_weights: bfloat16 [32, 1536, 4096], P('expert', None, 'dp'), may hold values from -0.15625 to 0.15625
Outputs:
- arrived: bfloat16 [2, 256, 4096], P('section', 'expert', 'dp')
The draws below stay inside these ranges and needn't reach their ends.
Inputs may be any that keep to these rules, and one draw needn't show every extreme that they name: `routes`: each token names 8 different experts. Among the 64 tokens of one device (aligned blocks of 64 tokens), no expert is named more than 16 times, and in some blocks one expert is named exactly 16 times.
All inputs are finite; a program needn't handle non-finite values.
Results may differ from the reference program's by a relative error of at most 0.005.
Values may be sent and summed in bfloat16 or wider, within the bound.
No kernel may reach another device: no remote copies, remote signals or barrier semaphores. Data moves between devices by JAX's collectives and lax.ppermute only.
A program may use at most 128 MiB of HBM per device.

```python
import math
import jax
import jax.numpy as jnp
import numpy as np
from jax import lax

D = 4096
FF = 1536
TOP = 8
TOK_DEV = 64
EXPERTS = 32
CAP = 16
TOKENS = 256
N_EXPERT = 4


def levels(key, extent, cuts, least, high):
    loudness = 1.0
    for axis_at, blocks in cuts:
        draws = jax.random.uniform(jax.random.fold_in(jax.random.fold_in(key, 6), axis_at), (blocks,), jnp.float32, least / len(cuts), high / len(cuts))
        loudness = loudness * jnp.repeat(jnp.exp(draws), extent[axis_at] // blocks).reshape((-1,) + (1,) * (len(extent) - 1 - axis_at))
    return loudness


def shared_out(stream_key, own, number, rows, amount, top, limit, skew):
    ranking = jax.random.permutation(stream_key, amount)
    crowded, usual = shares(amount, rows * top, limit, skew, True), shares(amount, rows * top, limit, skew, False)
    places = jnp.arange(amount)

    def named(tallies, turn):
        used = int((tallies > 0).sum())
        fixed = max(1, used // 4)
        passed = fixed + (places - fixed + turn * (used - fixed)) % max(1, amount - fixed)
        return jnp.zeros((amount,), jnp.int32).at[ranking[jnp.where(places < fixed, places, passed)]].set(jnp.asarray(tallies, jnp.int32))

    tallies = jnp.where(number % 4 == 0, named(crowded, number // 4), named(usual, number - number // 4 - 1))
    mixed = jax.random.permutation(jax.random.fold_in(own, 3), amount)
    source_of, taker = mixed[0:amount // 2 * 2:2], mixed[1:amount // 2 * 2:2]
    room = jnp.minimum(tallies[source_of] - 1, limit - tallies[taker]) // 2
    room = jnp.where((source_of == ranking[0]) | (taker == ranking[0]) | (tallies[taker] == 0), 0, jnp.maximum(room, 0))
    passed = jax.random.randint(jax.random.fold_in(own, 4), (amount // 2,), 0, 1 << 20) % (room + 1)
    tallies = tallies.at[source_of].add(-passed).at[taker].add(passed)
    labels = jnp.searchsorted(jnp.cumsum(tallies), jnp.arange(rows * top), side="right").astype(jnp.int32)
    table = labels.reshape(top, rows).T
    table = table[jax.random.permutation(jax.random.fold_in(own, 1), rows)]
    turn = jax.random.randint(jax.random.fold_in(own, 2), (rows, 1), 0, top)
    return jnp.take_along_axis(table, (jnp.arange(top)[None, :] + turn) % top, axis=1)


def shares(amount, total, bound, lean, full):
    loads = [(1 << 20) // math.isqrt(grade ** lean) + 1 for grade in range(1, amount + 1)]
    largest = bound if full else min(bound, max(-(-total // amount), total * loads[0] // sum(loads)))
    least = 1 if total - largest >= amount - 1 else 0
    counts, surplus = [largest] + [least] * (amount - 1), total - largest - least * (amount - 1)
    while surplus > 0:
        movable = [i for i in range(1, amount) if counts[i] < largest] or [i for i in range(1, amount) if counts[i] < bound]
        mass, left = sum([loads[i] for i in movable]), surplus
        for i in movable:
            addition = min(bound - counts[i], max(1, left * loads[i] // mass), surplus)
            counts[i] = counts[i] + addition
            surplus = surplus - addition
    return np.array(counts)


def normal_values(rng, shape, width, bound, pieces=(), kind=jnp.bfloat16):
    level = levels(rng, shape, pieces, -0.22, 0.18) if pieces else 1.0
    result = jax.random.normal(rng, shape, jnp.float32) * width * level
    return jnp.minimum(jnp.maximum(result, -bound), bound).astype(kind)


def setup_inputs(seed: int = 0) -> dict:
    streams_of = jax.random.split(jax.random.key(seed), 7)
    activations = normal_values(streams_of[0], (2, TOKENS, D), 1.0, 6.0, ((0, 2), (1, 4)))
    routes_keys = jax.random.split(jax.random.fold_in(streams_of[1], 1), 2 * TOKENS // TOK_DEV)
    routes_turns = jax.random.permutation(jax.random.fold_in(streams_of[1], 3), 2 * TOKENS // TOK_DEV)
    routes = jax.vmap(lambda own, number: shared_out(jax.random.fold_in(streams_of[1], 2), own, number, TOK_DEV, EXPERTS, TOP, CAP, 2))(routes_keys, routes_turns).reshape((2, TOKENS, TOP))
    gate_weights = jnp.clip(jnp.exp(math.log(0.5) - 2.3025851 * jax.random.uniform(streams_of[2], (2, TOKENS, TOP), jnp.float32) ** levels(streams_of[2], (2, TOKENS, TOP), ((0, 2), (1, 4)), -0.2, 0.2)), 0.05, 0.5)
    norm_gain = jnp.clip(1.0 + 0.18 * jax.random.normal(streams_of[3], (D,), jnp.float32), 0.099609375, 1.8984375).astype(jnp.bfloat16)
    gate_up_weights = normal_values(streams_of[4], (EXPERTS, 2, FF, D), D ** -0.5, 0.09375, ((0, 4), (2, 4)))
    down_weights = normal_values(streams_of[5], (EXPERTS, FF, D), FF ** -0.5, 0.15625, ((0, 4), (2, 4)))
    return dict(activations=activations, routes=routes, gate_weights=gate_weights, norm_gain=norm_gain, gate_up_weights=gate_up_weights, down_weights=down_weights)


def normalize(values, norm_gain):
    widened = values.astype(jnp.float32)
    mean_square = lax.optimization_barrier(jnp.mean(widened * widened, axis=-1, keepdims=True))
    return (widened * lax.rsqrt(mean_square + 1e-06) * norm_gain.astype(jnp.float32)).astype(jnp.bfloat16)

def expert_apply(packed):
    slot_rows, in_weights, out_weights = packed
    contract = (((1,), (1,)), ((), ()))
    gate_val = lax.dot_general(slot_rows, in_weights[0], contract, preferred_element_type=jnp.float32)
    up_val = lax.dot_general(slot_rows, in_weights[1], contract, preferred_element_type=jnp.float32)
    hidden_act = (jax.nn.silu(gate_val) * up_val).astype(jnp.bfloat16)
    return jnp.dot(hidden_act, out_weights, preferred_element_type=jnp.float32).astype(jnp.bfloat16)

def layer_apply(activations, routes, gate_weights, norm_gain, gate_up_weights, down_weights):
    normed = normalize(activations, norm_gain)
    token_count = activations.shape[0]
    flat_routes = routes.reshape(-1).astype(jnp.int32)
    experts_iota = jnp.arange(EXPERTS, dtype=jnp.int32)
    onehot = (flat_routes[:, None] == experts_iota[None, :]).astype(jnp.int32)
    slot_ranks = lax.optimization_barrier(jnp.sum((jnp.cumsum(onehot, axis=0) - onehot) * onehot, axis=1)).astype(jnp.int32)
    owners = jnp.arange(flat_routes.shape[0], dtype=jnp.int32) // TOP
    slot_depth = N_EXPERT * CAP
    buffers = jnp.zeros((EXPERTS, slot_depth, D), jnp.bfloat16).at[flat_routes, slot_ranks].set(normed[owners])
    results = lax.map(expert_apply, (buffers, gate_up_weights, down_weights))
    picked = results[flat_routes, slot_ranks].reshape(token_count, TOP, D).astype(jnp.float32)
    branch = lax.optimization_barrier(jnp.sum(picked * gate_weights.astype(jnp.float32)[:, :, None], axis=1))
    return (activations.astype(jnp.float32) + branch).astype(jnp.bfloat16)

def reference(activations, routes, gate_weights, norm_gain, gate_up_weights, down_weights):
    from_first = layer_apply(activations[0], routes[0], gate_weights[0], norm_gain, gate_up_weights, down_weights)
    second = layer_apply(activations[1], routes[1], gate_weights[1], norm_gain, gate_up_weights, down_weights)
    return jnp.stack([second, from_first])
```

```python
import functools

import jax
import jax.numpy as jnp
from jax import lax
from jax.experimental import pallas as pl
from jax.experimental.pallas import tpu as pltpu
from jax.sharding import PartitionSpec as P

CONTRACT_LAST = (((1,), (1,)), ((), ()))
IN_VMEM = pl.BlockSpec(memory_space=pltpu.VMEM)
IN_SMEM = pl.BlockSpec(memory_space=pltpu.SMEM)
ANYWHERE = pl.BlockSpec(memory_space=pl.ANY)
MIB = 1 << 20


def params(mib):
    return pltpu.CompilerParams(vmem_limit_bytes=mib * MIB)


def cost(flops, moved):
    return pl.CostEstimate(flops=int(flops), bytes_accessed=int(moved), transcendentals=0)


def pinned(array):
    return pltpu.with_memory_space_constraint(array, pltpu.VMEM)


def shifted(block, axis, distance):
    count = lax.axis_size(axis)
    return lax.ppermute(block, axis, [((i - distance) % count, i) for i in range(count)])


def flipped(block, axis, bit):
    return lax.ppermute(block, axis, [(i, i ^ bit) for i in range(lax.axis_size(axis))])


def norm_kernel(place, tokens, gain, normed, own):
    widened = tokens[...].astype(jnp.float32)
    mean_square = jnp.mean(widened * widened, axis=-1, keepdims=True)
    rows = widened * lax.rsqrt(mean_square + 1e-06) * gain[...].astype(jnp.float32)
    normed[...] = rows.astype(jnp.bfloat16)
    width = own.shape[1]
    start = pl.multiple_of(place[0] * width, width)
    own[...] = normed[:, pl.ds(start, width)]


def normalize(place, tokens, gain, width):
    count, features = tokens.shape
    return pl.pallas_call(
        norm_kernel,
        out_shape=(
            jax.ShapeDtypeStruct((count, features), jnp.bfloat16),
            jax.ShapeDtypeStruct((count, width), jnp.bfloat16),
        ),
        in_specs=[IN_SMEM, IN_VMEM, IN_VMEM],
        out_specs=(IN_VMEM, IN_VMEM),
        compiler_params=params(6),
    )(place, tokens, gain)


def plan_kernel(capacity, blocks, *refs):
    first = refs[0]
    routes = refs[1 : 1 + blocks]
    weights = refs[1 + blocks : 1 + 2 * blocks]
    placing, high, low = refs[1 + 2 * blocks :]
    tokens, top = routes[0].shape
    slots = placing.shape[1]
    lane = lax.broadcasted_iota(jnp.int32, (tokens, slots), 1)
    expert = first[0] + lane // capacity
    rank_of_lane = lane % capacity
    row = lax.broadcasted_iota(jnp.int32, (tokens, tokens), 0)
    column = lax.broadcasted_iota(jnp.int32, (tokens, tokens), 1)
    earlier = jnp.where(column < row, 1.0, 0.0).astype(jnp.bfloat16)
    for block in range(blocks):
        named = jnp.zeros((tokens, slots), jnp.float32)
        weight = jnp.zeros((tokens, slots), jnp.float32)
        for k in range(top):
            hit = routes[block][:, k : k + 1] == expert
            named = jnp.where(hit, 1.0, named)
            weight = jnp.where(hit, weights[block][:, k : k + 1], weight)
        ranks = jnp.dot(earlier, named.astype(jnp.bfloat16), preferred_element_type=jnp.float32)
        here = jnp.where((named > 0.5) & (ranks.astype(jnp.int32) == rank_of_lane), 1.0, 0.0)
        placing[block] = here.T.astype(jnp.bfloat16)
        scaled = here * weight
        coarse = scaled.astype(jnp.bfloat16)
        high[block] = coarse
        low[block] = (scaled - coarse.astype(jnp.float32)).astype(jnp.bfloat16)


def plan(first, routes, weights, slots, capacity):
    blocks, tokens = len(routes), routes[0].shape[0]
    return pl.pallas_call(
        functools.partial(plan_kernel, capacity, blocks),
        out_shape=(
            jax.ShapeDtypeStruct((blocks, slots, tokens), jnp.bfloat16),
            jax.ShapeDtypeStruct((blocks, tokens, slots), jnp.bfloat16),
            jax.ShapeDtypeStruct((blocks, tokens, slots), jnp.bfloat16),
        ),
        in_specs=[IN_SMEM] + [IN_VMEM] * (2 * blocks),
        out_specs=(IN_VMEM,) * 3,
        compiler_params=params(6),
    )(first, *routes, *weights)


def up_part(weights, target, semaphore, place, quarter):
    width = target.shape[-1]
    start = pl.multiple_of((place ^ quarter) * width, width)
    return pltpu.make_async_copy(weights.at[:, :, :, pl.ds(start, width)], target, semaphore)


def down_part(weights, target, semaphore, place, quarter):
    rows = target.shape[1]
    start = pl.multiple_of((place ^ quarter) * rows, rows)
    return pltpu.make_async_copy(weights.at[:, pl.ds(start, rows), :], target, semaphore)


def stage_kernel(quarters, place, weights, *refs):
    targets, semaphores = refs[: len(quarters)], refs[-1]
    copies = [
        up_part(weights, targets[i], semaphores.at[i], place[0], quarter)
        for i, quarter in enumerate(quarters)
    ]
    for copy in copies:
        copy.start()
    for copy in copies:
        copy.wait()


def stage(place, weights, quarters, width):
    shape = weights.shape[:-1] + (width,)
    count = len(quarters)
    return pl.pallas_call(
        functools.partial(stage_kernel, quarters),
        out_shape=(pltpu.VMEM(shape, weights.dtype),) * count,
        in_specs=[IN_SMEM, ANYWHERE],
        out_specs=(IN_VMEM,) * count,
        scratch_shapes=[pltpu.SemaphoreType.DMA((count,))],
        compiler_params=params(4),
        cost_estimate=cost(0, 2 * count * weights.size // 2),
    )(place, weights)


def up_kernel(opts, place, placing, normed, arrived, weights, *refs):
    quarter, has_total, finish, fetch_up, fetch_down, experts = opts
    refs = list(refs)
    total_in = refs.pop(0) if has_total else None
    up_source = refs.pop(0) if fetch_up else None
    down_source = refs.pop(0) if fetch_down else None
    result = refs.pop(0)
    up_targets = [refs.pop(0) for _ in fetch_up]
    down_targets = [refs.pop(0) for _ in fetch_down]
    gathered, rows = refs.pop(0), refs.pop(0)
    copies = []
    if fetch_up or fetch_down:
        semaphores = refs.pop(0)
        for i, part in enumerate(fetch_up):
            copies.append(up_part(up_source, up_targets[i], semaphores.at[i], place[0], part))
        for i, part in enumerate(fetch_down):
            at = semaphores.at[len(fetch_up) + i]
            copies.append(down_part(down_source, down_targets[i], at, place[0], part))
    for copy in copies:
        copy.start()
    blocks, slots, tokens = placing.shape
    local_experts, _, hidden, width = weights.shape
    capacity = slots // local_experts
    start = pl.multiple_of((place[0] ^ quarter) * width, width)
    rows[0:tokens] = normed[:, pl.ds(start, width)]
    rows[tokens:] = arrived[...]
    for block in range(blocks):
        picked = jnp.dot(
            placing[block],
            rows[block * tokens : (block + 1) * tokens],
            preferred_element_type=jnp.float32,
        ).astype(jnp.bfloat16)
        gathered[:, block * capacity : (block + 1) * capacity, :] = picked.reshape(
            local_experts, capacity, width
        )

    def one(expert, carry):
        own = gathered[expert]
        parts = []
        for side in range(2):
            value = lax.dot_general(
                own, weights[expert, side], CONTRACT_LAST, preferred_element_type=jnp.float32
            )
            if has_total:
                value = value + total_in[expert, side]
            parts.append(value)
        if finish:
            gate, up = parts
            result[expert - experts[0]] = (gate / (1.0 + jnp.exp(-gate)) * up).astype(jnp.bfloat16)
        else:
            result[expert, 0] = parts[0]
            result[expert, 1] = parts[1]
        return carry

    lax.fori_loop(experts[0], experts[1], one, 0)
    for copy in copies:
        copy.wait()


def up_step(place, placing, normed, arrived, weights, total, quarter, finish, experts, up=None, down=None):
    fetch_up, up_source = up if up else ((), None)
    fetch_down, down_source = down if down else ((), None)
    blocks, slots, tokens = placing.shape
    local_experts, _, hidden, width = weights.shape
    depth = blocks * (slots // local_experts)
    operands = [place, placing, normed, arrived, pinned(weights)]
    in_specs = [IN_SMEM] + [IN_VMEM] * 4
    if total is not None:
        operands.append(pinned(total))
        in_specs.append(IN_VMEM)
    if fetch_up:
        operands.append(up_source)
        in_specs.append(ANYWHERE)
    if fetch_down:
        operands.append(down_source)
        in_specs.append(ANYWHERE)
    count = experts[1] - experts[0]
    if finish:
        shapes = [jax.ShapeDtypeStruct((count, depth, hidden), jnp.bfloat16)]
    else:
        shapes = [pltpu.VMEM((local_experts, 2, depth, hidden), jnp.float32)]
    shapes += [pltpu.VMEM(weights.shape, weights.dtype) for _ in fetch_up]
    if fetch_down:
        shapes += [
            pltpu.VMEM((local_experts, hidden, down_source.shape[2]), down_source.dtype)
            for _ in fetch_down
        ]
    scratch = [
        pltpu.VMEM((local_experts, depth, width), jnp.bfloat16),
        pltpu.VMEM((blocks * tokens, width), jnp.bfloat16),
    ]
    copies = len(fetch_up) + len(fetch_down)
    if copies:
        scratch.append(pltpu.SemaphoreType.DMA((copies,)))
    return pl.pallas_call(
        functools.partial(
            up_kernel, (quarter, total is not None, finish, fetch_up, fetch_down, experts)
        ),
        out_shape=tuple(shapes),
        in_specs=in_specs,
        out_specs=(IN_VMEM,) * len(shapes),
        scratch_shapes=scratch,
        compiler_params=params(8),
        cost_estimate=cost(2 * count * 256 * 2 * hidden * width, 2 * weights.size),
    )(*operands)


def down_kernel(opts, *refs):
    has_total, last, pieces, local_experts = opts
    refs = list(refs)
    acts = [refs.pop(0) for _ in range(pieces)]
    weights = [refs.pop(0) for _ in range(pieces)]
    total_in = refs.pop(0) if has_total else None
    if last:
        high, low, tokens, place = [refs.pop(0) for _ in range(4)]
        results = [refs.pop(0) for _ in range(high.shape[0])]
        slots_out = refs.pop(0)
    else:
        result = refs.pop(0)

    def one(expert, carry):
        value = None
        for i in range(pieces):
            part = jnp.dot(acts[i][expert], weights[i][expert], preferred_element_type=jnp.float32)
            value = part if value is None else value + part
        if has_total:
            value = value + total_in[expert]
        if last:
            blocks = slots_out.shape[0]
            capacity = value.shape[0] // blocks
            rounded = value.astype(jnp.bfloat16)
            for block in range(blocks):
                at = pl.ds(pl.multiple_of(expert * capacity, capacity), capacity)
                slots_out[block, at, :] = rounded[block * capacity : (block + 1) * capacity]
        else:
            result[expert] = value
        return carry

    lax.fori_loop(0, local_experts, one, 0)
    if last:
        width = tokens.shape[1] // (tokens.shape[1] // slots_out.shape[2])
        start = pl.multiple_of(place[0] * width, width)
        for block in range(len(results)):
            value = jnp.dot(
                high[block], slots_out[block], preferred_element_type=jnp.float32
            ) + jnp.dot(low[block], slots_out[block], preferred_element_type=jnp.float32)
            if block == 0:
                value = value + tokens[:, pl.ds(start, width)].astype(jnp.float32)
            results[block][...] = value.astype(jnp.bfloat16)


def down_step(acts, weights, total, finish=None):
    pieces = len(acts)
    local_experts, depth, hidden = acts[0].shape
    width = weights[0].shape[2]
    operands = list(acts) + [pinned(w) for w in weights]
    if total is not None:
        operands.append(pinned(total))
    in_specs = [IN_VMEM] * len(operands)
    scratch = []
    if finish:
        high, low, tokens, place = finish
        operands += [high, low, tokens, place]
        in_specs += [IN_VMEM] * 3 + [IN_SMEM]
        blocks, count, slots = high.shape
        shapes = (jax.ShapeDtypeStruct((count, width), jnp.bfloat16),) * blocks
        scratch = [pltpu.VMEM((blocks, slots, width), jnp.bfloat16)]
    else:
        shapes = pltpu.VMEM((local_experts, depth, width), jnp.float32)
    return pl.pallas_call(
        functools.partial(
            down_kernel, (total is not None, finish is not None, pieces, local_experts)
        ),
        out_shape=shapes,
        in_specs=in_specs,
        out_specs=(IN_VMEM,) * len(shapes) if finish else IN_VMEM,
        scratch_shapes=scratch,
        compiler_params=params(8),
        cost_estimate=cost(
            2 * pieces * local_experts * 256 * hidden * width, 2 * pieces * weights[0].size
        ),
    )(*operands)


def sum_kernel(*refs):
    *parts, result = refs
    value = parts[0][...].astype(jnp.float32)
    for part in parts[1:]:
        value = value + part[...].astype(jnp.float32)
    result[0] = value.astype(jnp.bfloat16)


def gathered_tokens(activations, routes, gate_weights, norm_gain, gate_up_weights, down_weights):
    tokens = activations[0]
    token_count, features = tokens.shape
    local_experts = gate_up_weights.shape[0]
    rows = lax.axis_size("expert")
    dp_devices = lax.axis_size("dp")
    sections = lax.axis_size("section")
    capacity = token_count * routes.shape[2] // (local_experts * rows)
    slots = local_experts * capacity
    width = features // dp_devices
    place = lax.axis_index("dp").astype(jnp.int32).reshape(1)
    first = (lax.axis_index("expert") * local_experts).astype(jnp.int32).reshape(1)

    all_routes = [routes[0]] + [shifted(routes[0], "expert", j) for j in range(1, rows)]
    all_weights = [gate_weights[0]] + [
        shifted(gate_weights[0], "expert", j) for j in range(1, rows)
    ]
    normed, own = normalize(place, tokens, norm_gain.reshape(1, features), width)
    blocks = [shifted(own, "expert", j) for j in range(1, rows)]
    placing, high, low = plan(first, all_routes, all_weights, slots, capacity)
    staged_0, staged_1 = stage(place, gate_up_weights, (0, 1), width)

    mine = jnp.concatenate(blocks, axis=0)
    across = flipped(mine, "dp", 2)
    beside = flipped(mine, "dp", 1)
    everyone = (0, local_experts)
    half = local_experts // 2
    step = functools.partial(up_step, place, placing, normed)
    total, staged_2 = step(
        mine, staged_0, None, 0, False, everyone, up=((2,), gate_up_weights)
    )
    total, staged_3 = step(
        beside, staged_1, total, 1, False, everyone, up=((3,), gate_up_weights)
    )
    total, down_0, down_1 = step(
        across, staged_2, total, 2, False, everyone, down=((0, 1), down_weights)
    )
    far = flipped(across, "dp", 1)
    act, down_2, down_3 = step(
        far, staged_3, total, 3, True, everyone, down=((2, 3), down_weights)
    )

    act_across = flipped(act, "dp", 2)
    act_beside = flipped(act, "dp", 1)
    act_far = flipped(act_across, "dp", 1)
    summed = down_step([act, act_beside], [down_0, down_1], None)
    partial = down_step(
        [act_across, act_far], [down_2, down_3], summed, (high, low, tokens, place)
    )
    received = []
    for j in range(rows):
        route = [
            (s * rows + e, ((s + 1) % sections) * rows + (e - j) % rows)
            for s in range(sections)
            for e in range(rows)
        ]
        received.append(lax.ppermute(partial[j], ("section", "expert"), route))
    return pl.pallas_call(
        sum_kernel,
        out_shape=jax.ShapeDtypeStruct((1, token_count, width), jnp.bfloat16),
        in_specs=[IN_VMEM] * rows,
        out_specs=IN_VMEM,
        compiler_params=params(6),
    )(*received)

def routed_rows(activations, routes, gate_weights, norm_gain, gate_up_weights, down_weights):
    tokens_here = activations[0]
    token_count, feature_count = tokens_here.shape
    top_count = routes.shape[2]
    local_experts = gate_up_weights.shape[0]
    expert_devices = lax.axis_size("expert")
    dp_devices = lax.axis_size("dp")
    total_experts = local_experts * expert_devices
    window = max(1, token_count * top_count // (total_experts * dp_devices))
    capacity = window * dp_devices
    slice_width = feature_count // dp_devices
    dp_place = lax.axis_index("dp")
    widened = tokens_here.astype(jnp.float32)
    mean_square = jnp.mean(widened * widened, axis=-1, keepdims=True)
    normed = (widened * lax.rsqrt(mean_square + 1e-06) * norm_gain.astype(jnp.float32)).astype(
        jnp.bfloat16
    )
    flat_routes = routes[0].reshape(-1)
    experts_iota = jnp.arange(total_experts, dtype=jnp.int32)
    onehot = (flat_routes[:, None] == experts_iota[None, :]).astype(jnp.int32)
    slot_ranks = jnp.sum((jnp.cumsum(onehot, axis=0) - onehot) * onehot, axis=1)
    targets = flat_routes * capacity + slot_ranks
    contract_rows = (((0,), (0,)), ((), ()))
    slot_iota = jnp.arange(total_experts * capacity, dtype=jnp.int32)
    matches = (targets[:, None] == slot_iota[None, :]).reshape(
        token_count, top_count, total_experts * capacity
    )
    placing = jnp.any(matches, axis=1).astype(jnp.bfloat16)
    normed_slice = lax.dynamic_slice_in_dim(normed, dp_place * slice_width, slice_width, 1)
    outgoing = lax.dot_general(
        placing, normed_slice, contract_rows, preferred_element_type=jnp.float32
    )
    outgoing = outgoing.astype(jnp.bfloat16).reshape(total_experts, capacity, slice_width)
    arriving = lax.all_to_all(outgoing, "expert", split_axis=0, concat_axis=0, tiled=True)
    arriving = arriving.reshape(expert_devices, local_experts, capacity, slice_width)
    weights_part = gate_up_weights
    gate_up = jnp.einsum(
        "seck,ejhk->jsech",
        lax.all_gather(arriving, "dp", axis=3, tiled=True),
        weights_part,
        preferred_element_type=jnp.float32,
    )
    hidden_act = (jax.nn.silu(gate_up[0]) * gate_up[1]).astype(jnp.bfloat16)
    weights_part = down_weights
    summed = jnp.einsum(
        "sech,ehf->secf",
        lax.all_gather(hidden_act, "dp", axis=3, tiled=True),
        weights_part,
        preferred_element_type=jnp.float32,
    )
    expert_out = summed.astype(jnp.bfloat16)
    returned = lax.all_to_all(expert_out, "expert", split_axis=0, concat_axis=0, tiled=True)
    returned_flat = returned.reshape(total_experts * capacity, slice_width)
    picked = jnp.take(returned_flat, targets, axis=0).reshape(token_count, top_count, slice_width)
    branch = jnp.sum(picked.astype(jnp.float32) * gate_weights[0][:, :, None], axis=1)
    residual = lax.dynamic_slice_in_dim(widened, dp_place * slice_width, slice_width, 1)
    finished = (residual + branch).astype(jnp.bfloat16)
    arrived = shifted(finished, "section", 1)
    return arrived[None]


def body(activations, routes, gate_weights, norm_gain, gate_up_weights, down_weights):
    token_count, top_count = routes.shape[1], routes.shape[2]
    local_experts = gate_up_weights.shape[0]
    rows = lax.axis_size("expert")
    capacity = token_count * top_count // (local_experts * rows)
    few = token_count <= local_experts * capacity
    aligned = capacity % 16 == 0 and token_count % 16 == 0
    form = gathered_tokens if few and aligned and lax.axis_size("dp") == 4 else routed_rows
    return form(
        activations, routes, gate_weights, norm_gain, gate_up_weights, down_weights
    )


def solution(mesh):
    placed = (
        P("section", "expert", None),
        P("section", "expert", None),
        P("section", "expert", None),
        P(),
        P("expert", None, "dp", None),
        P("expert", None, "dp"),
    )
    return jax.shard_map(
        body, mesh=mesh, in_specs=placed, out_specs=P("section", "expert", "dp"), check_vma=False
    )
```

```python
import functools

import jax
import jax.numpy as jnp
from jax import lax
from jax.experimental import pallas as pl
from jax.experimental.pallas import tpu as pltpu
from jax.sharding import PartitionSpec as P

CONTRACT_LAST = (((1,), (1,)), ((), ()))
IN_VMEM = pl.BlockSpec(memory_space=pltpu.VMEM)
IN_SMEM = pl.BlockSpec(memory_space=pltpu.SMEM)
IN_HBM = pl.BlockSpec(memory_space=pltpu.HBM)
MIB = 1 << 20
LANES = 128


def params(mib):
    return pltpu.CompilerParams(vmem_limit_bytes=mib * MIB)


def cost(flops, moved):
    return pl.CostEstimate(flops=int(flops), bytes_accessed=int(moved), transcendentals=0)


def pinned(array):
    return pltpu.with_memory_space_constraint(array, pltpu.VMEM)


def in_hbm(array):
    return pltpu.with_memory_space_constraint(array, pltpu.HBM)


def shifted(block, axis, distance):
    count = lax.axis_size(axis)
    return lax.ppermute(block, axis, [((i - distance) % count, i) for i in range(count)])


def flipped(block, axis, bit):
    return lax.ppermute(block, axis, [(i, i ^ bit) for i in range(lax.axis_size(axis))])


def norm_kernel(ids, *refs):
    sources, (normed, sent), landed, semaphores = refs[:4], refs[4:6], refs[6:10], refs[10]
    copies = [
        pltpu.make_async_copy(source, target, semaphores.at[i])
        for i, (source, target) in enumerate(zip(sources, landed))
    ]
    for copy in copies:
        copy.start()
    for copy in copies:
        copy.wait()
    tokens, gain, routes, weights = landed
    widened = tokens[...].astype(jnp.float32)
    mean_square = jnp.mean(widened * widened, axis=-1, keepdims=True)
    rows = widened * lax.rsqrt(mean_square + 1e-06)
    rows = rows * gain[...].astype(jnp.float32).reshape(1, rows.shape[1])
    normed[...] = rows.astype(jnp.bfloat16)
    count, features = normed.shape
    pieces = sent.shape[0] // count
    start = pl.multiple_of(ids[0] * pieces * LANES, pieces * LANES)
    for i in range(pieces):
        at = pl.ds(pl.multiple_of(start + i * LANES, LANES), LANES)
        sent[i * count : (i + 1) * count] = normed[:, at]
    whole = weights[...]
    coarse = whole.astype(jnp.bfloat16).astype(jnp.float32)
    middle = (whole - coarse).astype(jnp.bfloat16).astype(jnp.float32)
    fine = whole - coarse - middle
    upper = jnp.concatenate([routes[...].astype(jnp.float32), coarse])
    lower = jnp.concatenate([middle, fine])
    sent[pieces * count :] = jnp.concatenate([upper, lower], axis=1).astype(jnp.bfloat16)


def normalize(ids, tokens, gain, routes, weights, width):
    count, features = tokens.shape
    top = routes.shape[0]
    operands = (tokens, gain, routes, weights)
    return pl.pallas_call(
        norm_kernel,
        out_shape=(
            jax.ShapeDtypeStruct((count, features), jnp.bfloat16),
            jax.ShapeDtypeStruct((count * width // LANES + 2 * top, LANES), jnp.bfloat16),
        ),
        in_specs=[IN_SMEM] + [IN_HBM] * 4,
        out_specs=(IN_VMEM, IN_VMEM),
        scratch_shapes=[pltpu.VMEM(x.shape, x.dtype) for x in operands]
        + [pltpu.SemaphoreType.DMA((4,))],
        compiler_params=params(8),
    )(ids, *(in_hbm(x) for x in operands))


def relay_kernel(block, after, result):
    result[...] = block[...]


def relayed(block, after):
    return pl.pallas_call(
        relay_kernel,
        out_shape=jax.ShapeDtypeStruct(block.shape, block.dtype),
        in_specs=[IN_VMEM, IN_VMEM],
        out_specs=IN_VMEM,
        compiler_params=params(8),
    )(block, after)


def collect_kernel(*refs):
    *blocks, staged, result = refs
    count = result.shape[0] // len(blocks)
    for i, block in enumerate(blocks):
        for j in range(result.shape[1] // LANES):
            result[i * count : (i + 1) * count, j * LANES : (j + 1) * LANES] = block[
                j * count : (j + 1) * count
            ]


def collect(blocks, count, width, staged):
    return pl.pallas_call(
        collect_kernel,
        out_shape=jax.ShapeDtypeStruct((len(blocks) * count, width), jnp.bfloat16),
        in_specs=[IN_VMEM] * (len(blocks) + 1),
        out_specs=IN_VMEM,
        compiler_params=params(8),
    )(*blocks, pinned(staged))


def plan_kernel(capacity, top, ids, *refs):
    blocks = refs[:-3]
    placing, high, low = refs[-3:]
    tokens, slots = high.shape[1:]
    lane = lax.broadcasted_iota(jnp.int32, (tokens, slots), 1)
    expert = (ids[1] + lane // capacity).astype(jnp.float32)
    rank_of_lane = lane % capacity
    row = lax.broadcasted_iota(jnp.int32, (tokens, tokens), 0)
    column = lax.broadcasted_iota(jnp.int32, (tokens, tokens), 1)
    earlier = jnp.where(column < row, 1.0, 0.0).astype(jnp.bfloat16)
    for i, block in enumerate(blocks):
        named = jnp.zeros((tokens, slots), jnp.float32)
        weight = jnp.zeros((tokens, slots), jnp.float32)
        sent = block[block.shape[0] - 2 * top :].astype(jnp.float32)
        sent = jnp.concatenate(
            [
                sent[:, :tokens],
                sent[:, LANES // 2 : LANES // 2 + tokens],
                jnp.zeros((LANES - 4 * top, tokens), jnp.float32),
            ]
        ).T
        for k in range(top):
            hit = sent[:, k : k + 1] == expert
            value = sum(sent[:, part * top + k : part * top + k + 1] for part in (1, 2, 3))
            named = jnp.where(hit, 1.0, named)
            weight = jnp.where(hit, value, weight)
        ranks = jnp.dot(earlier, named.astype(jnp.bfloat16), preferred_element_type=jnp.float32)
        here = jnp.where((named > 0.5) & (ranks.astype(jnp.int32) == rank_of_lane), 1.0, 0.0)
        placing[i] = here.T.astype(jnp.bfloat16)
        scaled = here * weight
        coarse = scaled.astype(jnp.bfloat16)
        high[i] = coarse
        low[i] = (scaled - coarse.astype(jnp.float32)).astype(jnp.bfloat16)


def plan(ids, blocks, tokens, slots, capacity, top):
    count = len(blocks)
    return pl.pallas_call(
        functools.partial(plan_kernel, capacity, top),
        out_shape=(
            jax.ShapeDtypeStruct((count, slots, tokens), jnp.bfloat16),
            jax.ShapeDtypeStruct((count, tokens, slots), jnp.bfloat16),
            jax.ShapeDtypeStruct((count, tokens, slots), jnp.bfloat16),
        ),
        in_specs=[IN_SMEM] + [IN_VMEM] * count,
        out_specs=(IN_VMEM,) * 3,
        compiler_params=params(8),
    )(ids, *blocks)


def up_part(weights, store, semaphores, place, expert, slot, quarter):
    width = store.shape[-1]
    start = pl.multiple_of((place ^ quarter) * width, width)
    source = weights.at[expert, :, :, pl.ds(start, width)]
    return [pltpu.make_async_copy(source, store.at[slot, expert], semaphores.at[slot, 0, expert])]


def down_part(weights, store, semaphores, place, expert, slot):
    rows = store.shape[-2]
    copies = []
    for side in range(2):
        start = pl.multiple_of((place ^ (2 * slot + side)) * rows, rows)
        source = weights.at[expert, pl.ds(start, rows), :]
        target = store.at[slot, expert, side]
        copies.append(pltpu.make_async_copy(source, target, semaphores.at[slot, side, expert]))
    return copies


def stage_kernel(ids, weights, store, semaphores):
    slots, local_experts = store.shape[:2]
    copies = [
        copy
        for slot in range(slots)
        for expert in range(local_experts)
        for copy in up_part(weights, store, semaphores, ids[0], expert, slot, slot)
    ]
    for copy in copies:
        copy.start()
    for copy in copies:
        copy.wait()


def stage(ids, weights, width):
    shape = (2,) + weights.shape[:-1] + (width,)
    return pl.pallas_call(
        stage_kernel,
        out_shape=pltpu.VMEM(shape, weights.dtype),
        in_specs=[IN_SMEM, IN_HBM],
        out_specs=IN_VMEM,
        scratch_shapes=[pltpu.SemaphoreType.DMA((2, 1, weights.shape[0]))],
        compiler_params=params(8),
        cost_estimate=cost(0, weights.size),
    )(ids, in_hbm(weights))


def refill(source, store, semaphores, place, expert, quarters, down):
    copies = []
    for quarter in quarters:
        slot = quarter % 2
        if down:
            copies += down_part(source, store, semaphores, place, expert, slot)
        else:
            copies += up_part(source, store, semaphores, place, expert, slot, quarter + 2)
    return copies


def up_kernel(opts, ids, placing, normed, *refs):
    quarters, has_total, finish, experts, late = opts
    refs = list(refs)
    arrived = [refs.pop(0) for _ in quarters]
    total_in = refs.pop(0) if has_total else None
    source, before, _, result, store, gathered, rows, semaphores, at_start = refs
    blocks, slots, tokens = placing.shape
    _, local_experts, _, hidden, width = store.shape
    capacity = slots // local_experts
    place = ids[0]
    first_copies = []
    if late:
        for expert in late[0]:
            first_copies += refill(before, store, at_start, place, expert, late[1], late[2])
    for copy in first_copies:
        copy.start()

    for i, quarter in enumerate(quarters):
        start = pl.multiple_of((place ^ quarter) * width, width)
        rows[0:tokens] = normed[:, pl.ds(start, width)]
        rows[tokens:] = arrived[i][...]
        for block in range(blocks):
            picked = jnp.dot(
                placing[block, experts[0] * capacity : experts[1] * capacity],
                rows[block * tokens : (block + 1) * tokens],
                preferred_element_type=jnp.float32,
            ).astype(jnp.bfloat16)
            at = slice(block * capacity, (block + 1) * capacity)
            gathered[i, :, at, :] = picked.reshape(experts[1] - experts[0], capacity, width)

    def pair(first):
        for expert in (first, first + 1):
            value = total_in[expert] if has_total else None
            for i, quarter in enumerate(quarters):
                part = lax.dot_general(
                    gathered[i, expert - experts[0]],
                    store[quarter % 2, expert].reshape(2 * hidden, width),
                    CONTRACT_LAST,
                    preferred_element_type=jnp.float32,
                )
                value = part if value is None else value + part
            if finish:
                gate, up = value[:, :hidden], value[:, hidden:]
                value = (gate / (1.0 + jnp.exp(-gate)) * up).astype(jnp.bfloat16)
                result[expert - experts[0]] = value
            else:
                result[expert] = value

    def replaced(expert):
        return refill(source, store, semaphores, place, expert, quarters, finish)

    def some(step, carry):
        first = experts[0] + 2 * step
        pair(first)

        @pl.when(step < (experts[1] - experts[0]) // 2 - 1)
        def _():
            for expert in (first, first + 1):
                for copy in replaced(expert):
                    copy.start()

        return carry

    lax.fori_loop(0, (experts[1] - experts[0]) // 2, some, 0)
    for expert in range(experts[0], experts[1] - 2):
        for copy in replaced(expert):
            copy.wait()
    for copy in first_copies:
        copy.wait()


def up_step(ids, placing, normed, arrived, total, quarters, finish, experts, source, before, late, store):
    blocks, slots, tokens = placing.shape
    _, local_experts, _, hidden, width = store.shape
    depth = blocks * (slots // local_experts)
    operands = [ids, placing, normed] + list(arrived)
    if total is not None:
        operands.append(total)
    operands += [in_hbm(source), in_hbm(before), pinned(store)]
    in_specs = [IN_SMEM] + [IN_VMEM] * (len(operands) - 4) + [IN_HBM, IN_HBM, IN_VMEM]
    count = experts[1] - experts[0]
    if finish:
        shape = jax.ShapeDtypeStruct((count, depth, hidden), jnp.bfloat16)
    else:
        shape = jax.ShapeDtypeStruct((local_experts, depth, 2 * hidden), jnp.float32)
    return pl.pallas_call(
        functools.partial(up_kernel, (quarters, total is not None, finish, experts, late)),
        out_shape=(shape, pltpu.VMEM(store.shape, store.dtype)),
        in_specs=in_specs,
        out_specs=(IN_VMEM, IN_VMEM),
        input_output_aliases={len(operands) - 1: 1},
        scratch_shapes=[
            pltpu.VMEM((len(quarters), count, depth, width), jnp.bfloat16),
            pltpu.VMEM((blocks * tokens, width), jnp.bfloat16),
            pltpu.SemaphoreType.DMA((2, 2, local_experts)),
            pltpu.SemaphoreType.DMA((2, 2, local_experts)),
        ],
        compiler_params=params(8),
        cost_estimate=cost(0, 3 * source.size // 4),
    )(*operands)


def down_kernel(groups, pieces, has_total, late, *refs):
    refs = list(refs)
    acts = [[refs.pop(0) for _ in group] for group in pieces]
    total_in = refs.pop(0) if has_total else None
    copies = []
    if late:
        ids, source, _, result, store, semaphores = refs
        for expert in late:
            copies += refill(source, store, semaphores, ids[0], expert, (2, 3), True)
        for copy in copies:
            copy.start()
    else:
        store, result = refs

    def one(group, index, carry):
        expert = groups[group][0] + index
        value = total_in[expert] if has_total else None
        for act, q in zip(acts[group], pieces[group]):
            weights = store[q // 2, expert, q % 2]
            part = jnp.dot(act[index], weights, preferred_element_type=jnp.float32)
            value = part if value is None else value + part
        result[expert] = value
        return carry

    for group, (low, high) in enumerate(groups):
        if group == len(groups) - 1:
            for copy in copies:
                copy.wait()
        lax.fori_loop(0, high - low, functools.partial(one, group), 0, unroll=2)


def down_step(groups, acts, store, total, late=None):
    pieces = [tuple(sorted(group)) for group in acts]
    _, local_experts, _, hidden, width = store.shape
    depth = acts[0][pieces[0][0]].shape[1]
    operands = [group[q] for group, piece in zip(acts, pieces) for q in piece]
    in_specs = [IN_VMEM] * len(operands)
    aliases, scratch = {}, []
    if total is not None:
        aliases = {len(operands): 0}
        operands.append(total)
        in_specs.append(IN_VMEM)
    shapes = (jax.ShapeDtypeStruct((local_experts, depth, width), jnp.float32),)
    if late:
        experts, ids, source = late
        operands += [ids, in_hbm(source)]
        in_specs += [IN_SMEM, IN_HBM]
        aliases[len(operands)] = 1
        shapes += (pltpu.VMEM(store.shape, store.dtype),)
        scratch = [pltpu.SemaphoreType.DMA((2, 2, local_experts))]
    operands.append(pinned(store))
    in_specs.append(IN_VMEM)
    return pl.pallas_call(
        functools.partial(
            down_kernel, groups, pieces, total is not None, experts if late else None
        ),
        out_shape=shapes,
        in_specs=in_specs,
        out_specs=(IN_VMEM,) * len(shapes),
        input_output_aliases=aliases,
        scratch_shapes=scratch,
        compiler_params=params(8),
        cost_estimate=cost(0, store.size // 2),
    )(*operands)


def finish_kernel(opts, ids, *refs):
    group, quarters, part, parts = opts
    refs = list(refs)
    acts = [refs.pop(0) for _ in quarters]
    store, total, high, low, tokens = [refs.pop(0) for _ in range(5)]
    kept, given, slots_out = refs
    local_experts, depth, whole = total.shape
    width = whole // parts
    lanes = slice(part * width, (part + 1) * width)
    blocks = high.shape[0]
    capacity = depth // blocks

    def place(expert, value):
        rounded = value.astype(jnp.bfloat16)
        at = pl.ds(pl.multiple_of(expert * capacity, capacity), capacity)
        for block in range(blocks):
            slots_out[block, at, :] = rounded[block * capacity : (block + 1) * capacity]

    def known(expert, carry):
        place(expert, total[expert, :, lanes])
        return carry

    def one(expert, carry):
        value = total[expert, :, lanes]
        for act, q in zip(acts, quarters):
            weights = store[q // 2, expert, q % 2, :, lanes]
            value = value + jnp.dot(
                act[expert - group[0]], weights, preferred_element_type=jnp.float32
            )
        place(expert, value)
        return carry

    lax.fori_loop(0, group[0], known, 0)
    lax.fori_loop(group[0], group[1], one, 0)
    start = pl.multiple_of(ids[0] * whole + part * width, LANES)
    for block in range(blocks):
        value = jnp.dot(
            high[block], slots_out[block], preferred_element_type=jnp.float32
        ) + jnp.dot(low[block], slots_out[block], preferred_element_type=jnp.float32)
        if block == 0:
            value = value + tokens[:, pl.ds(start, width)].astype(jnp.float32)
        target = given if block % 2 else kept
        target[block // 2] = value.astype(jnp.bfloat16)


def finish_step(ids, group, acts, store, total, high, low, tokens, part, parts):
    quarters = tuple(sorted(acts))
    blocks, count, slots = high.shape
    width = total.shape[2] // parts
    operands = [ids] + [acts[q] for q in quarters]
    operands += [pinned(store), total, high, low, tokens]
    shape = jax.ShapeDtypeStruct((blocks // 2, count, width), jnp.bfloat16)
    return pl.pallas_call(
        functools.partial(finish_kernel, (group, quarters, part, parts)),
        out_shape=(shape, shape),
        in_specs=[IN_SMEM] + [IN_VMEM] * (len(operands) - 1),
        out_specs=(IN_VMEM, IN_VMEM),
        scratch_shapes=[pltpu.VMEM((blocks, slots, width), jnp.bfloat16)],
        compiler_params=params(8),
        cost_estimate=cost(0, store.size // 8),
    )(*operands)


def add_kernel(own, other, *results):
    size = own.shape[0] // len(results)
    for i, result in enumerate(results):
        for j in range(size):
            value = own[j * len(results) + i].astype(jnp.float32)
            value = value + other[j * len(results) + i].astype(jnp.float32)
            result[j] = value.astype(jnp.bfloat16)


def add_up(own, other):
    count = own.shape[0]
    sides = min(2, count)
    shape = jax.ShapeDtypeStruct((count // sides,) + own.shape[1:], own.dtype)
    return pl.pallas_call(
        add_kernel,
        out_shape=(shape,) * sides,
        in_specs=[IN_VMEM, IN_VMEM],
        out_specs=(IN_VMEM,) * sides,
        compiler_params=params(8),
    )(own, other)


def sum_kernel(*refs):
    *parts, result = refs
    width = parts[0].shape[2]
    for i in range(result.shape[2] // width):
        value = parts[2 * i][0].astype(jnp.float32) + parts[2 * i + 1][0].astype(jnp.float32)
        result[0, :, i * width : (i + 1) * width] = value.astype(jnp.bfloat16)


def gathered_tokens(activations, routes, gate_weights, norm_gain, gate_up_weights, down_weights):
    tokens = activations[0]
    token_count, features = tokens.shape
    local_experts = gate_up_weights.shape[0]
    rows = lax.axis_size("expert")
    dp_devices = lax.axis_size("dp")
    sections = lax.axis_size("section")
    capacity = token_count * routes.shape[2] // (local_experts * rows)
    slots = local_experts * capacity
    width = features // dp_devices
    ids = jnp.stack([lax.axis_index("dp"), lax.axis_index("expert") * local_experts])
    ids = ids.astype(jnp.int32)

    normed, own = normalize(ids, tokens, norm_gain, routes[0].T, gate_weights[0].T, width)
    blocks = [flipped(own, "expert", j) for j in range(1, rows)]
    store = stage(ids, gate_up_weights, width)
    mine = collect(blocks, token_count, width, store)
    across = flipped(mine, "dp", 2)
    beside = flipped(mine, "dp", 1)
    placing, high, low = plan(
        ids, [own] + blocks, token_count, slots, capacity, routes.shape[2]
    )
    everyone = (0, local_experts)
    half = local_experts // 2
    groups = ((0, half), (half, local_experts))
    step = functools.partial(up_step, ids, placing, normed)
    wide, tall = gate_up_weights, down_weights
    left = (local_experts - 2, local_experts - 1)
    total, store = step([mine], None, (0,), False, everyone, wide, wide, None, store)
    across = relayed(across, total)
    far = flipped(across, "dp", 1)
    late = (left, (0,), False)
    total, store = step([beside], total, (1,), False, everyone, wide, wide, late, store)
    step = functools.partial(step, [across, far], total, (2, 3), True)
    late = (left, (1,), False)
    act, store = step(groups[0], tall, wide, late, store)
    acts = [{0: act, 1: flipped(act, "dp", 1), 2: flipped(act, "dp", 2)}]
    late = ((half - 2, half - 1), (2, 3), True)
    act, store = step(groups[1], tall, tall, late, store)
    acts.append({0: act, 1: flipped(act, "dp", 1), 2: flipped(act, "dp", 2)})
    near = [{q: act[q] for q in (0, 1)} for act in acts]
    summed, store = down_step(groups, near, store, None, (left, ids, tall))
    middle = relayed(acts[0][2], summed)
    middle = {2: middle, 3: flipped(middle, "dp", 1)}
    (summed,) = down_step(groups[:1], [middle], store, summed)
    last = relayed(acts[1][2], summed)
    last = {2: last, 3: flipped(last, "dp", 1)}
    parts = 2
    received = []
    for part in range(parts):
        kept, given = finish_step(
            ids, groups[1], last, store, summed, high, low, tokens, part, parts
        )
        near, given = add_up(kept, flipped(given, "expert", 1))
        for block, j in ((given, 2), (near, 0)):
            route = [
                (s * rows + e, ((s + 1) % sections) * rows + (e ^ j))
                for s in range(sections)
                for e in range(rows)
            ]
            received.append(lax.ppermute(block, ("section", "expert"), route))
    return pl.pallas_call(
        sum_kernel,
        out_shape=jax.ShapeDtypeStruct((1, token_count, width), jnp.bfloat16),
        in_specs=[IN_VMEM] * len(received),
        out_specs=IN_VMEM,
        compiler_params=params(8),
    )(*received)


def routed_rows(activations, routes, gate_weights, norm_gain, gate_up_weights, down_weights):
    tokens_here = activations[0]
    token_count, feature_count = tokens_here.shape
    top_count = routes.shape[2]
    local_experts = gate_up_weights.shape[0]
    expert_devices = lax.axis_size("expert")
    dp_devices = lax.axis_size("dp")
    total_experts = local_experts * expert_devices
    window = max(1, token_count * top_count // (total_experts * dp_devices))
    capacity = window * dp_devices
    slice_width = feature_count // dp_devices
    dp_place = lax.axis_index("dp")
    widened = tokens_here.astype(jnp.float32)
    mean_square = jnp.mean(widened * widened, axis=-1, keepdims=True)
    normed = (widened * lax.rsqrt(mean_square + 1e-06) * norm_gain.astype(jnp.float32)).astype(
        jnp.bfloat16
    )
    flat_routes = routes[0].reshape(-1)
    experts_iota = jnp.arange(total_experts, dtype=jnp.int32)
    onehot = (flat_routes[:, None] == experts_iota[None, :]).astype(jnp.int32)
    slot_ranks = jnp.sum((jnp.cumsum(onehot, axis=0) - onehot) * onehot, axis=1)
    targets = flat_routes * capacity + slot_ranks
    contract_rows = (((0,), (0,)), ((), ()))
    slot_iota = jnp.arange(total_experts * capacity, dtype=jnp.int32)
    matches = (targets[:, None] == slot_iota[None, :]).reshape(
        token_count, top_count, total_experts * capacity
    )
    placing = jnp.any(matches, axis=1).astype(jnp.bfloat16)
    normed_slice = lax.dynamic_slice_in_dim(normed, dp_place * slice_width, slice_width, 1)
    outgoing = lax.dot_general(
        placing, normed_slice, contract_rows, preferred_element_type=jnp.float32
    )
    outgoing = outgoing.astype(jnp.bfloat16).reshape(total_experts, capacity, slice_width)
    arriving = lax.all_to_all(outgoing, "expert", split_axis=0, concat_axis=0, tiled=True)
    arriving = arriving.reshape(expert_devices, local_experts, capacity, slice_width)
    weights_part = gate_up_weights
    gate_up = jnp.einsum(
        "seck,ejhk->jsech",
        lax.all_gather(arriving, "dp", axis=3, tiled=True),
        weights_part,
        preferred_element_type=jnp.float32,
    )
    hidden_act = (jax.nn.silu(gate_up[0]) * gate_up[1]).astype(jnp.bfloat16)
    weights_part = down_weights
    summed = jnp.einsum(
        "sech,ehf->secf",
        lax.all_gather(hidden_act, "dp", axis=3, tiled=True),
        weights_part,
        preferred_element_type=jnp.float32,
    )
    expert_out = summed.astype(jnp.bfloat16)
    returned = lax.all_to_all(expert_out, "expert", split_axis=0, concat_axis=0, tiled=True)
    returned_flat = returned.reshape(total_experts * capacity, slice_width)
    picked = jnp.take(returned_flat, targets, axis=0).reshape(token_count, top_count, slice_width)
    branch = jnp.sum(picked.astype(jnp.float32) * gate_weights[0][:, :, None], axis=1)
    residual = lax.dynamic_slice_in_dim(widened, dp_place * slice_width, slice_width, 1)
    finished = (residual + branch).astype(jnp.bfloat16)
    arrived = shifted(finished, "section", 1)
    return arrived[None]


def body(activations, routes, gate_weights, norm_gain, gate_up_weights, down_weights):
    token_count, top_count = routes.shape[1], routes.shape[2]
    local_experts = gate_up_weights.shape[0]
    rows = lax.axis_size("expert")
    capacity = token_count * top_count // (local_experts * rows)
    few = token_count <= local_experts * capacity
    aligned = capacity % 16 == 0 and token_count % 16 == 0
    suits = rows == 4 and lax.axis_size("dp") == 4 and token_count * 2 == LANES
    form = gathered_tokens if few and aligned and suits else routed_rows
    return form(
        activations, routes, gate_weights, norm_gain, gate_up_weights, down_weights
    )


def solution(mesh):
    placed = (
        P("section", "expert", None),
        P("section", "expert", None),
        P("section", "expert", None),
        P(),
        P("expert", None, "dp", None),
        P("expert", None, "dp"),
    )
    return jax.shard_map(
        body, mesh=mesh, in_specs=placed, out_specs=P("section", "expert", "dp"), check_vma=False
    )
```

```python
import functools

import jax
import jax.numpy as jnp
from jax import lax
from jax.experimental import pallas as pl
from jax.experimental.pallas import tpu as pltpu
from jax.sharding import PartitionSpec as P

CONTRACT_LAST = (((1,), (1,)), ((), ()))
IN_VMEM = pl.BlockSpec(memory_space=pltpu.VMEM)
IN_SMEM = pl.BlockSpec(memory_space=pltpu.SMEM)
IN_HBM = pl.BlockSpec(memory_space=pltpu.HBM)
MIB = 1 << 20
LANES = 128
SPARE = 1


def params(mib):
    return pltpu.CompilerParams(vmem_limit_bytes=mib * MIB)


def cost(flops, moved):
    return pl.CostEstimate(flops=int(flops), bytes_accessed=int(moved), transcendentals=0)


def pinned(array):
    return pltpu.with_memory_space_constraint(array, pltpu.VMEM)


def in_hbm(array):
    return pltpu.with_memory_space_constraint(array, pltpu.HBM)


def shifted(block, axis, distance):
    count = lax.axis_size(axis)
    return lax.ppermute(block, axis, [((i - distance) % count, i) for i in range(count)])


def flipped(block, axis, bit):
    return lax.ppermute(block, axis, [(i, i ^ bit) for i in range(lax.axis_size(axis))])


def norm_kernel(ids, *refs):
    sources, (normed, sent), landed, semaphores = refs[:4], refs[4:6], refs[6:10], refs[10]
    copies = [
        pltpu.make_async_copy(source, target, semaphores.at[i])
        for i, (source, target) in enumerate(zip(sources, landed))
    ]
    for copy in copies:
        copy.start()
    for copy in copies:
        copy.wait()
    tokens, gain, routes, weights = landed
    widened = tokens[...].astype(jnp.float32)
    mean_square = jnp.mean(widened * widened, axis=-1, keepdims=True)
    rows = widened * lax.rsqrt(mean_square + 1e-06)
    rows = rows * gain[...].astype(jnp.float32).reshape(1, rows.shape[1])
    normed[...] = rows.astype(jnp.bfloat16)
    count, features = normed.shape
    pieces = sent.shape[0] // count
    start = pl.multiple_of(ids[0] * pieces * LANES, pieces * LANES)
    for i in range(pieces):
        at = pl.ds(pl.multiple_of(start + i * LANES, LANES), LANES)
        sent[i * count : (i + 1) * count] = normed[:, at]
    whole = weights[...]
    coarse = whole.astype(jnp.bfloat16).astype(jnp.float32)
    middle = (whole - coarse).astype(jnp.bfloat16).astype(jnp.float32)
    fine = whole - coarse - middle
    upper = jnp.concatenate([routes[...].astype(jnp.float32), coarse])
    lower = jnp.concatenate([middle, fine])
    sent[pieces * count :] = jnp.concatenate([upper, lower], axis=1).astype(jnp.bfloat16)


def normalize(ids, tokens, gain, routes, weights, width):
    count, features = tokens.shape
    top = routes.shape[0]
    operands = (tokens, gain, routes, weights)
    return pl.pallas_call(
        norm_kernel,
        out_shape=(
            jax.ShapeDtypeStruct((count, features), jnp.bfloat16),
            jax.ShapeDtypeStruct((count * width // LANES + 2 * top, LANES), jnp.bfloat16),
        ),
        in_specs=[IN_SMEM] + [IN_HBM] * 4,
        out_specs=(IN_VMEM, IN_VMEM),
        scratch_shapes=[pltpu.VMEM(x.shape, x.dtype) for x in operands]
        + [pltpu.SemaphoreType.DMA((4,))],
        compiler_params=params(5),
    )(ids, *(in_hbm(x) for x in operands))


def relay_kernel(block, after, result):
    result[...] = block[...]


def relayed(block, after):
    return pl.pallas_call(
        relay_kernel,
        out_shape=jax.ShapeDtypeStruct(block.shape, block.dtype),
        in_specs=[IN_VMEM, IN_VMEM],
        out_specs=IN_VMEM,
        compiler_params=params(5),
        cost_estimate=cost(0, MIB),
    )(block, after)


def collect_kernel(*refs):
    *blocks, staged, result = refs
    count = result.shape[0] // len(blocks)
    for i, block in enumerate(blocks):
        for j in range(result.shape[1] // LANES):
            result[i * count : (i + 1) * count, j * LANES : (j + 1) * LANES] = block[
                j * count : (j + 1) * count
            ]


def collect(blocks, count, width, staged):
    return pl.pallas_call(
        collect_kernel,
        out_shape=jax.ShapeDtypeStruct((len(blocks) * count, width), jnp.bfloat16),
        in_specs=[IN_VMEM] * (len(blocks) + 1),
        out_specs=IN_VMEM,
        compiler_params=params(5),
    )(*blocks, pinned(staged))


def write_plan(capacity, top, first_expert, blocks, placing, high, low):
    tokens, slots = high.shape[1:]
    count = len(blocks) * tokens
    lane = lax.broadcasted_iota(jnp.int32, (count, slots), 1)
    expert = (first_expert + lane // capacity).astype(jnp.float32)
    rank_of_lane = (lane % capacity).astype(jnp.float32)
    row = lax.broadcasted_iota(jnp.int32, (tokens, tokens), 0)
    column = lax.broadcasted_iota(jnp.int32, (tokens, tokens), 1)
    earlier = jnp.where(column < row, 1.0, 0.0).astype(jnp.bfloat16)
    sent = [block[block.shape[0] - 2 * top :].astype(jnp.float32) for block in blocks]
    upper = jnp.concatenate([part[:, :tokens] for part in sent], axis=1)
    lower = jnp.concatenate([part[:, LANES // 2 : LANES // 2 + tokens] for part in sent], axis=1)
    names = upper[:top]
    values = upper[top:] + lower[:top] + lower[top:]
    rest = jnp.zeros((LANES - 2 * top, count), jnp.float32)
    table = jnp.concatenate([names, values, rest]).T
    weight = jnp.zeros((count, slots), jnp.float32)
    for k in range(top):
        hit = table[:, k : k + 1] == expert
        weight = jnp.where(hit, table[:, top + k : top + k + 1], weight)
    named = jnp.where(weight > 0, 1.0, 0.0)
    for i in range(len(blocks)):
        own = slice(i * tokens, (i + 1) * tokens)
        ranks = jnp.dot(earlier, named[own].astype(jnp.bfloat16), preferred_element_type=jnp.float32)
        fits = (named[own] > 0) & (ranks == rank_of_lane[own])
        placing[i] = jnp.where(fits, 1.0, 0.0).T.astype(jnp.bfloat16)
        scaled = jnp.where(fits, weight[own], 0.0)
        coarse = scaled.astype(jnp.bfloat16)
        high[i] = coarse
        low[i] = (scaled - coarse.astype(jnp.float32)).astype(jnp.bfloat16)


def ring_place(store, kind, expert):
    _, places, _, _, _ = store.shape
    local_experts = places - SPARE
    return (kind * local_experts + expert) % places


def moves_of(store, moves):
    cut = []
    for when, kind, first, count, slot in moves:
        for expert in range(first, first + count):
            if expert > first and ring_place(store, kind, expert) > 0:
                cut[-1][3] += 1
            else:
                cut.append([when, kind, expert, 1, slot])
    return cut


def move(wide, tall, store, semaphore, place, kind, first, count, slot):
    experts = pl.ds(first, count)
    if kind == 2:
        source = tall.at[experts, pl.ds(2 * ((place >> 1) ^ slot), 2)]
    else:
        width = store.shape[-1]
        start = pl.multiple_of((place ^ (2 * kind + slot)) * width, width)
        source = wide.at[experts, :, :, pl.ds(start, width)]
    target = store.at[slot, pl.ds(ring_place(store, kind, first), count)]
    return pltpu.make_async_copy(source, target, semaphore)


def down_at(store, place, quarter, expert):
    return quarter // 2, ring_place(store, 2, expert), (quarter ^ place) & 1


def stage_kernel(ids, wide, tall, store, semaphores):
    count = store.shape[1] - SPARE
    copies = [
        move(wide, tall, store, semaphores.at[slot], ids[0], 0, 0, count, slot) for slot in range(2)
    ]
    for copy in copies:
        copy.start()
    for copy in copies:
        copy.wait()


def stage(ids, wide, tall, width):
    shape = (2, wide.shape[0] + SPARE) + wide.shape[1:-1] + (width,)
    return pl.pallas_call(
        stage_kernel,
        out_shape=pltpu.VMEM(shape, wide.dtype),
        in_specs=[IN_SMEM, IN_HBM, IN_HBM],
        out_specs=IN_VMEM,
        scratch_shapes=[pltpu.SemaphoreType.DMA((2,))],
        compiler_params=params(5),
        cost_estimate=cost(0, wide.size),
    )(ids, in_hbm(wide), in_hbm(tall))


def up_kernel(opts, ids, *refs):
    quarters, experts, total_first, finish, planned, moves = opts
    refs = list(refs)
    if planned:
        top, payloads = planned[0], [refs.pop(0) for _ in range(planned[1])]
    else:
        placing = refs.pop(0)
    normed = refs.pop(0)
    arrived = [refs.pop(0) for _ in quarters]
    total_in = refs.pop(0) if total_first is not None else None
    wide, tall, _, result, store = [refs.pop(0) for _ in range(5)]
    if planned:
        placing, high, low = [refs.pop(0) for _ in range(3)]
    gathered, rows, semaphores = refs
    blocks, slots, tokens = placing.shape
    _, places, _, hidden, width = store.shape
    capacity = slots // (places - SPARE)
    place = ids[0]
    copies = [
        move(wide, tall, store, semaphores.at[i], place, *what)
        for i, (_, *what) in enumerate(moves)
    ]
    for copy, (when, *_) in zip(copies, moves):
        if when is None:
            copy.start()
    if planned:
        write_plan(capacity, top, ids[1], payloads, placing, high, low)
    for i, quarter in enumerate(quarters):
        start = pl.multiple_of((place ^ quarter) * width, width)
        rows[0:tokens] = normed[:, pl.ds(start, width)]
        rows[tokens:] = arrived[i][...]
        for block in range(blocks):
            picked = jnp.dot(
                placing[block, experts[0] * capacity : experts[1] * capacity],
                rows[block * tokens : (block + 1) * tokens],
                preferred_element_type=jnp.float32,
            ).astype(jnp.bfloat16)
            at = slice(block * capacity, (block + 1) * capacity)
            gathered[i, :, at, :] = picked.reshape(experts[1] - experts[0], capacity, width)

    for expert in range(*experts):
        for copy, (when, *_) in zip(copies, moves):
            if when == expert:
                copy.start()
        value = total_in[expert - total_first] if total_in is not None else None
        for i, quarter in enumerate(quarters):
            part = lax.dot_general(
                gathered[i, expert - experts[0]],
                store[quarter % 2, ring_place(store, quarter // 2, expert)].reshape(2 * hidden, width),
                CONTRACT_LAST,
                preferred_element_type=jnp.float32,
            )
            value = part if value is None else value + part
        if finish:
            gate, up = value[:, :hidden], value[:, hidden:]
            value = (gate / (1.0 + jnp.exp(-gate)) * up).astype(jnp.bfloat16)
        result[expert - experts[0]] = value
    for copy in copies:
        copy.wait()


def up_step(ids, plan, normed, arrived, total, quarters, finish, experts, moves, wide, tall, store):
    _, places, _, hidden, width = store.shape
    moves = moves_of(store, moves)
    if isinstance(plan, dict):
        planned = (plan["top"], len(plan["payloads"]))
        blocks, slots, tokens = plan["shape"]
        operands = [ids] + list(plan["payloads"])
    else:
        planned = None
        blocks, slots, tokens = plan.shape
        operands = [ids, plan]
    depth = blocks * (slots // (places - SPARE))
    operands += [normed] + list(arrived)
    total_first = None
    if total is not None:
        total_first = total[1]
        operands.append(total[0])
    in_specs = [IN_SMEM] + [IN_VMEM] * (len(operands) - 1) + [IN_HBM, IN_HBM, IN_VMEM]
    operands += [in_hbm(wide), in_hbm(tall), pinned(store)]
    count = experts[1] - experts[0]
    if finish:
        shape = jax.ShapeDtypeStruct((count, depth, hidden), jnp.bfloat16)
    else:
        shape = jax.ShapeDtypeStruct((count, depth, 2 * hidden), jnp.float32)
    shapes = (shape, pltpu.VMEM(store.shape, store.dtype))
    if planned:
        shapes += (jax.ShapeDtypeStruct((blocks, slots, tokens), jnp.bfloat16),)
        shapes += (jax.ShapeDtypeStruct((blocks, tokens, slots), jnp.bfloat16),) * 2
    opts = (quarters, experts, total_first, finish, planned, moves)
    return pl.pallas_call(
        functools.partial(up_kernel, opts),
        out_shape=shapes,
        in_specs=in_specs,
        out_specs=(IN_VMEM,) * len(shapes),
        input_output_aliases={len(operands) - 1: 1},
        scratch_shapes=[
            pltpu.VMEM((len(quarters), count, depth, width), jnp.bfloat16),
            pltpu.VMEM((blocks * tokens, width), jnp.bfloat16),
            pltpu.SemaphoreType.DMA((len(moves),)),
        ],
        compiler_params=params(5),
        cost_estimate=cost(0, wide.size * len(quarters) * count // 8),
    )(*operands)


def down_kernel(groups, pieces, has_total, moves, ids, *refs):
    refs = list(refs)
    acts = [[refs.pop(0) for _ in group] for group in pieces]
    total_in = refs.pop(0) if has_total else None
    copies = []
    if moves:
        wide, tall, _, result, store, semaphores = refs
        for i, (_, *what) in enumerate(moves):
            copies.append(move(wide, tall, store, semaphores.at[i], ids[0], *what))
        for copy in copies:
            copy.start()
    else:
        store, result = refs
    for group, (low, high) in enumerate(groups):
        for expert in range(low, high):
            for copy, (when, *_) in zip(copies, moves):
                if when == expert:
                    copy.wait()
            value = total_in[expert] if has_total else None
            for act, q in zip(acts[group], pieces[group]):
                weights = store[down_at(store, ids[0], q, expert)]
                part = jnp.dot(act[expert - low], weights, preferred_element_type=jnp.float32)
                value = part if value is None else value + part
            result[expert] = value
    for copy, (when, *_) in zip(copies, moves):
        if when is None:
            copy.wait()


def down_step(ids, groups, acts, store, total, moves=(), wide=None, tall=None):
    pieces = [tuple(sorted(group)) for group in acts]
    local_experts, width = store.shape[1] - SPARE, store.shape[-1]
    moves = moves_of(store, moves)
    depth = acts[0][pieces[0][0]].shape[1]
    operands = [ids] + [group[q] for group, piece in zip(acts, pieces) for q in piece]
    in_specs = [IN_SMEM] + [IN_VMEM] * (len(operands) - 1)
    aliases, scratch = {}, []
    if total is not None:
        aliases = {len(operands): 0}
        operands.append(total)
        in_specs.append(IN_VMEM)
    shapes = (jax.ShapeDtypeStruct((local_experts, depth, width), jnp.float32),)
    if moves:
        operands += [in_hbm(wide), in_hbm(tall)]
        in_specs += [IN_HBM, IN_HBM]
        aliases[len(operands)] = 1
        shapes += (pltpu.VMEM(store.shape, store.dtype),)
        scratch = [pltpu.SemaphoreType.DMA((len(moves),))]
    operands.append(pinned(store))
    in_specs.append(IN_VMEM)
    return pl.pallas_call(
        functools.partial(down_kernel, groups, pieces, total is not None, moves),
        out_shape=shapes,
        in_specs=in_specs,
        out_specs=(IN_VMEM,) * len(shapes),
        input_output_aliases=aliases,
        scratch_shapes=scratch,
        compiler_params=params(5),
        cost_estimate=cost(0, 4 * MIB * len(acts)),
    )(*operands)


def finish_kernel(opts, ids, *refs):
    groups, quarter, part, parts = opts
    refs = list(refs)
    acts = [refs.pop(0) for _ in groups]
    store, total, high, low, tokens = [refs.pop(0) for _ in range(5)]
    kept, given, slots_out = refs
    local_experts, depth, whole = total.shape
    width = whole // parts
    lanes = slice(part * width, (part + 1) * width)
    blocks = high.shape[0]
    capacity = depth // blocks

    def place(expert, value):
        rounded = value.astype(jnp.bfloat16)
        at = slice(expert * capacity, (expert + 1) * capacity)
        for block in range(blocks):
            slots_out[block, at, :] = rounded[block * capacity : (block + 1) * capacity]

    for act, group in zip(acts, groups):
        for expert in range(*group):
            weights = store[*down_at(store, ids[0], quarter, expert), :, lanes]
            part_sum = jnp.dot(act[expert - group[0]], weights, preferred_element_type=jnp.float32)
            place(expert, total[expert, :, lanes] + part_sum)
    start = pl.multiple_of(ids[0] * whole + part * width, LANES)
    for block in range(blocks):
        value = jnp.dot(
            high[block], slots_out[block], preferred_element_type=jnp.float32
        ) + jnp.dot(low[block], slots_out[block], preferred_element_type=jnp.float32)
        if block == 0:
            value = value + tokens[:, pl.ds(start, width)].astype(jnp.float32)
        target = given if block % 2 else kept
        target[block // 2] = value.astype(jnp.bfloat16)


def finish_step(ids, groups, acts, quarter, store, total, high, low, tokens, part, parts):
    blocks, count, slots = high.shape
    width = total.shape[2] // parts
    operands = [ids] + list(acts)
    operands += [pinned(store), total, high, low, tokens]
    shape = jax.ShapeDtypeStruct((blocks // 2, count, width), jnp.bfloat16)
    return pl.pallas_call(
        functools.partial(finish_kernel, (groups, quarter, part, parts)),
        out_shape=(shape, shape),
        in_specs=[IN_SMEM] + [IN_VMEM] * (len(operands) - 1),
        out_specs=(IN_VMEM, IN_VMEM),
        scratch_shapes=[pltpu.VMEM((blocks, slots, width), jnp.bfloat16)],
        compiler_params=params(5),
        cost_estimate=cost(0, 0),
    )(*operands)


def add_kernel(own, other, *results):
    size = own.shape[0] // len(results)
    for i, result in enumerate(results):
        for j in range(size):
            value = own[j * len(results) + i].astype(jnp.float32)
            value = value + other[j * len(results) + i].astype(jnp.float32)
            result[j] = value.astype(jnp.bfloat16)


def add_up(own, other):
    count = own.shape[0]
    sides = min(2, count)
    shape = jax.ShapeDtypeStruct((count // sides,) + own.shape[1:], own.dtype)
    return pl.pallas_call(
        add_kernel,
        out_shape=(shape,) * sides,
        in_specs=[IN_VMEM, IN_VMEM],
        out_specs=(IN_VMEM,) * sides,
        compiler_params=params(5),
    )(own, other)


def sum_kernel(*refs):
    *parts, result = refs
    width = parts[0].shape[2]
    for i in range(result.shape[2] // width):
        value = parts[2 * i][0].astype(jnp.float32) + parts[2 * i + 1][0].astype(jnp.float32)
        result[0, :, i * width : (i + 1) * width] = value.astype(jnp.bfloat16)


def gathered_tokens(activations, routes, gate_weights, norm_gain, gate_up_weights, down_weights):
    tokens = activations[0]
    token_count, features = tokens.shape
    local_experts = gate_up_weights.shape[0]
    rows = lax.axis_size("expert")
    dp_devices = lax.axis_size("dp")
    sections = lax.axis_size("section")
    capacity = token_count * routes.shape[2] // (local_experts * rows)
    slots = local_experts * capacity
    width = features // dp_devices
    ids = jnp.stack([lax.axis_index("dp"), lax.axis_index("expert") * local_experts])
    ids = ids.astype(jnp.int32)

    normed, own = normalize(ids, tokens, norm_gain, routes[0].T, gate_weights[0].T, width)
    blocks = [flipped(own, "expert", j) for j in range(1, rows)]
    wide = gate_up_weights
    tall = down_weights.reshape(local_experts, dp_devices, -1, width)
    store = stage(ids, wide, tall, width)
    mine = collect(blocks, token_count, width, store)
    across = flipped(mine, "dp", 2)
    beside = flipped(mine, "dp", 1)
    cut = local_experts - 3 * local_experts // 8
    first, second = groups = ((0, cut), (cut, local_experts))

    end = local_experts
    moves = [(None, 1, 0, 1, slot) for slot in range(2)]
    moves += [(e, 1, e - 1, 2, slot) for e in range(2, end, 2) for slot in range(2)][:-1]
    payload = {
        "payloads": [own] + blocks,
        "top": routes.shape[2],
        "shape": (rows, slots, token_count),
    }

    total, store, placing, high, low = up_step(
        ids, payload, normed, [mine, beside], None, (0, 1), False, (0, local_experts),
        moves, wide, tall, store,
    )
    across = relayed(across, total)
    far = flipped(across, "dp", 1)

    step = functools.partial(up_step, ids, placing, normed)
    moves = [(None, 1, end - 3, 2, 1), (None, 1, end - 1, 1, 0), (None, 2, 0, 1, 0)]
    partial, store = step([across], (total, 0), (2,), False, first, moves, wide, tall, store)
    moves = [(None, 1, end - 1, 1, 1), (None, 2, 1, cut - 1, 0)]
    act, store = step([far], (partial, 0), (3,), True, first, moves, wide, tall, store)
    acts = [{0: act, 1: flipped(act, "dp", 1), 2: flipped(act, "dp", 2)}]
    moves = [(None, 2, cut, 1, 0), (None, 2, 0, cut - 1, 1)]
    moves += [(e, 2, e, 1, 0) for e in range(cut + 1, end - 1)]
    act, store = step(
        [across, far], (total, 0), (2, 3), True, second, moves, wide, tall, store
    )
    acts.append({0: act, 1: flipped(act, "dp", 1), 2: flipped(act, "dp", 2)})
    near = [{q: acts[0][q] for q in (0, 1)}, {0: acts[1][0]}]
    moves = [(end - 1, 2, end - 1, 1, 0), (None, 2, cut - 1, end - cut + 1, 1)]
    summed, store = down_step(ids, groups, near, store, None, moves, wide, tall)
    middle = relayed(acts[0][2], summed)
    last = relayed(acts[1][2], middle)
    far = [flipped(act, "dp", 1) for act in (middle, last)]
    pieces = [{2: middle}, {1: acts[1][1], 2: last}]
    (summed,) = down_step(ids, groups, pieces, store, summed)
    parts = 2
    received = []
    for part in range(parts):
        kept, given = finish_step(
            ids, groups, far, 3, store, summed, high, low, tokens, part, parts
        )
        near, given = add_up(kept, flipped(given, "expert", 1))
        for block, j in ((given, 2), (near, 0)):
            route = [
                (s * rows + e, ((s + 1) % sections) * rows + (e ^ j))
                for s in range(sections)
                for e in range(rows)
            ]
            received.append(lax.ppermute(block, ("section", "expert"), route))
    return pl.pallas_call(
        sum_kernel,
        out_shape=jax.ShapeDtypeStruct((1, token_count, width), jnp.bfloat16),
        in_specs=[IN_VMEM] * len(received),
        out_specs=IN_VMEM,
        compiler_params=params(5),
    )(*received)


def routed_rows(activations, routes, gate_weights, norm_gain, gate_up_weights, down_weights):
    tokens_here = activations[0]
    token_count, feature_count = tokens_here.shape
    top_count = routes.shape[2]
    local_experts = gate_up_weights.shape[0]
    expert_devices = lax.axis_size("expert")
    dp_devices = lax.axis_size("dp")
    total_experts = local_experts * expert_devices
    window = max(1, token_count * top_count // (total_experts * dp_devices))
    capacity = window * dp_devices
    slice_width = feature_count // dp_devices
    dp_place = lax.axis_index("dp")
    widened = tokens_here.astype(jnp.float32)
    mean_square = jnp.mean(widened * widened, axis=-1, keepdims=True)
    normed = (widened * lax.rsqrt(mean_square + 1e-06) * norm_gain.astype(jnp.float32)).astype(
        jnp.bfloat16
    )
    flat_routes = routes[0].reshape(-1)
    experts_iota = jnp.arange(total_experts, dtype=jnp.int32)
    onehot = (flat_routes[:, None] == experts_iota[None, :]).astype(jnp.int32)
    slot_ranks = jnp.sum((jnp.cumsum(onehot, axis=0) - onehot) * onehot, axis=1)
    targets = flat_routes * capacity + slot_ranks
    contract_rows = (((0,), (0,)), ((), ()))
    slot_iota = jnp.arange(total_experts * capacity, dtype=jnp.int32)
    matches = (targets[:, None] == slot_iota[None, :]).reshape(
        token_count, top_count, total_experts * capacity
    )
    placing = jnp.any(matches, axis=1).astype(jnp.bfloat16)
    normed_slice = lax.dynamic_slice_in_dim(normed, dp_place * slice_width, slice_width, 1)
    outgoing = lax.dot_general(
        placing, normed_slice, contract_rows, preferred_element_type=jnp.float32
    )
    outgoing = outgoing.astype(jnp.bfloat16).reshape(total_experts, capacity, slice_width)
    arriving = lax.all_to_all(outgoing, "expert", split_axis=0, concat_axis=0, tiled=True)
    arriving = arriving.reshape(expert_devices, local_experts, capacity, slice_width)
    weights_part = gate_up_weights
    gate_up = jnp.einsum(
        "seck,ejhk->jsech",
        lax.all_gather(arriving, "dp", axis=3, tiled=True),
        weights_part,
        preferred_element_type=jnp.float32,
    )
    hidden_act = (jax.nn.silu(gate_up[0]) * gate_up[1]).astype(jnp.bfloat16)
    weights_part = down_weights
    summed = jnp.einsum(
        "sech,ehf->secf",
        lax.all_gather(hidden_act, "dp", axis=3, tiled=True),
        weights_part,
        preferred_element_type=jnp.float32,
    )
    expert_out = summed.astype(jnp.bfloat16)
    returned = lax.all_to_all(expert_out, "expert", split_axis=0, concat_axis=0, tiled=True)
    returned_flat = returned.reshape(total_experts * capacity, slice_width)
    picked = jnp.take(returned_flat, targets, axis=0).reshape(token_count, top_count, slice_width)
    branch = jnp.sum(picked.astype(jnp.float32) * gate_weights[0][:, :, None], axis=1)
    residual = lax.dynamic_slice_in_dim(widened, dp_place * slice_width, slice_width, 1)
    finished = (residual + branch).astype(jnp.bfloat16)
    arrived = shifted(finished, "section", 1)
    return arrived[None]


def body(activations, routes, gate_weights, norm_gain, gate_up_weights, down_weights):
    token_count, top_count = routes.shape[1], routes.shape[2]
    local_experts = gate_up_weights.shape[0]
    rows = lax.axis_size("expert")
    capacity = token_count * top_count // (local_experts * rows)
    few = token_count <= local_experts * capacity and local_experts % 8 == 0
    aligned = capacity % 16 == 0 and token_count % 16 == 0
    suits = rows == 4 and lax.axis_size("dp") == 4 and token_count * 2 == LANES
    form = gathered_tokens if few and aligned and suits else routed_rows
    return form(
        activations, routes, gate_weights, norm_gain, gate_up_weights, down_weights
    )


def solution(mesh):
    placed = (
        P("section", "expert", None),
        P("section", "expert", None),
        P("section", "expert", None),
        P(),
        P("expert", None, "dp", None),
        P("expert", None, "dp"),
    )
    return jax.shard_map(
        body, mesh=mesh, in_specs=placed, out_specs=P("section", "expert", "dp"), check_vma=False
    )
```

```python
import functools

import jax
import jax.numpy as jnp
from jax import lax
from jax.experimental import pallas as pl
from jax.experimental.pallas import tpu as pltpu
from jax.sharding import PartitionSpec as P

CONTRACT_LAST = (((1,), (1,)), ((), ()))
IN_VMEM = pl.BlockSpec(memory_space=pltpu.VMEM)
IN_SMEM = pl.BlockSpec(memory_space=pltpu.SMEM)
IN_HBM = pl.BlockSpec(memory_space=pltpu.HBM)
MIB = 1 << 20
LANES = 128
SPARE = 1


def params(mib):
    return pltpu.CompilerParams(vmem_limit_bytes=mib * MIB)


def cost(flops, moved):
    return pl.CostEstimate(flops=int(flops), bytes_accessed=int(moved), transcendentals=0)


def pinned(array):
    return pltpu.with_memory_space_constraint(array, pltpu.VMEM)


def in_hbm(array):
    return pltpu.with_memory_space_constraint(array, pltpu.HBM)


def shifted(block, axis, distance):
    count = lax.axis_size(axis)
    return lax.ppermute(block, axis, [((i - distance) % count, i) for i in range(count)])


def flipped(block, axis, bit):
    return lax.ppermute(block, axis, [(i, i ^ bit) for i in range(lax.axis_size(axis))])


def norm_kernel(ids, *refs):
    sources, (normed, sent), landed, semaphores = refs[:4], refs[4:6], refs[6:10], refs[10]
    copies = [
        pltpu.make_async_copy(source, target, semaphores.at[i])
        for i, (source, target) in enumerate(zip(sources, landed))
    ]
    for copy in copies:
        copy.start()
    for copy in copies:
        copy.wait()
    tokens, gain, routes, weights = landed
    widened = tokens[...].astype(jnp.float32)
    mean_square = jnp.mean(widened * widened, axis=-1, keepdims=True)
    rows = widened * lax.rsqrt(mean_square + 1e-06)
    rows = rows * gain[...].astype(jnp.float32).reshape(1, rows.shape[1])
    normed[...] = rows.astype(jnp.bfloat16)
    count, features = normed.shape
    pieces = sent.shape[0] // count
    start = pl.multiple_of(ids[0] * pieces * LANES, pieces * LANES)
    for i in range(pieces):
        at = pl.ds(pl.multiple_of(start + i * LANES, LANES), LANES)
        sent[i * count : (i + 1) * count] = normed[:, at]
    whole = weights[...]
    coarse = whole.astype(jnp.bfloat16).astype(jnp.float32)
    middle = (whole - coarse).astype(jnp.bfloat16).astype(jnp.float32)
    fine = whole - coarse - middle
    upper = jnp.concatenate([routes[...].astype(jnp.float32), coarse])
    lower = jnp.concatenate([middle, fine])
    sent[pieces * count :] = jnp.concatenate([upper, lower], axis=1).astype(jnp.bfloat16)


def normalize(ids, tokens, gain, routes, weights, width):
    count, features = tokens.shape
    top = routes.shape[0]
    operands = (tokens, gain, routes, weights)
    return pl.pallas_call(
        norm_kernel,
        out_shape=(
            jax.ShapeDtypeStruct((count, features), jnp.bfloat16),
            jax.ShapeDtypeStruct((count * width // LANES + 2 * top, LANES), jnp.bfloat16),
        ),
        in_specs=[IN_SMEM] + [IN_HBM] * 4,
        out_specs=(IN_VMEM, IN_VMEM),
        scratch_shapes=[pltpu.VMEM(x.shape, x.dtype) for x in operands]
        + [pltpu.SemaphoreType.DMA((4,))],
        compiler_params=params(5),
    )(ids, *(in_hbm(x) for x in operands))


def relay_kernel(block, after, result):
    result[...] = block[...]


def relayed(block, after):
    return pl.pallas_call(
        relay_kernel,
        out_shape=jax.ShapeDtypeStruct(block.shape, block.dtype),
        in_specs=[IN_VMEM, IN_VMEM],
        out_specs=IN_VMEM,
        compiler_params=params(5),
        cost_estimate=cost(0, MIB),
    )(block, after)


def collect_kernel(*refs):
    *blocks, staged, result = refs
    count = result.shape[0] // len(blocks)
    for i, block in enumerate(blocks):
        for j in range(result.shape[1] // LANES):
            result[i * count : (i + 1) * count, j * LANES : (j + 1) * LANES] = block[
                j * count : (j + 1) * count
            ]


def collect(blocks, count, width, staged):
    return pl.pallas_call(
        collect_kernel,
        out_shape=jax.ShapeDtypeStruct((len(blocks) * count, width), jnp.bfloat16),
        in_specs=[IN_VMEM] * (len(blocks) + 1),
        out_specs=IN_VMEM,
        compiler_params=params(5),
    )(*blocks, pinned(staged))


def write_plan(capacity, top, first_expert, blocks, placing, high, low):
    tokens, slots = high.shape[1:]
    count = len(blocks) * tokens
    lane = lax.broadcasted_iota(jnp.int32, (count, slots), 1)
    expert = (first_expert + lane // capacity).astype(jnp.float32)
    rank_of_lane = (lane % capacity).astype(jnp.float32)
    row = lax.broadcasted_iota(jnp.int32, (tokens, tokens), 0)
    column = lax.broadcasted_iota(jnp.int32, (tokens, tokens), 1)
    earlier = jnp.where(column < row, 1.0, 0.0).astype(jnp.bfloat16)
    sent = [block[block.shape[0] - 2 * top :].astype(jnp.float32) for block in blocks]
    upper = jnp.concatenate([part[:, :tokens] for part in sent], axis=1)
    lower = jnp.concatenate([part[:, LANES // 2 : LANES // 2 + tokens] for part in sent], axis=1)
    names = upper[:top]
    values = upper[top:] + lower[:top] + lower[top:]
    rest = jnp.zeros((LANES - 2 * top, count), jnp.float32)
    table = jnp.concatenate([names, values, rest]).T
    weight = jnp.zeros((count, slots), jnp.float32)
    for k in range(top):
        hit = table[:, k : k + 1] == expert
        weight = jnp.where(hit, table[:, top + k : top + k + 1], weight)
    named = jnp.where(weight > 0, 1.0, 0.0)
    for i in range(len(blocks)):
        own = slice(i * tokens, (i + 1) * tokens)
        ranks = jnp.dot(earlier, named[own].astype(jnp.bfloat16), preferred_element_type=jnp.float32)
        fits = (named[own] > 0) & (ranks == rank_of_lane[own])
        placing[i] = jnp.where(fits, 1.0, 0.0).T.astype(jnp.bfloat16)
        scaled = jnp.where(fits, weight[own], 0.0)
        coarse = scaled.astype(jnp.bfloat16)
        high[i] = coarse
        low[i] = (scaled - coarse.astype(jnp.float32)).astype(jnp.bfloat16)


def ring_place(store, kind, expert):
    _, places, _, _, _ = store.shape
    local_experts = places - SPARE
    return (kind * local_experts + expert) % places


def moves_of(store, moves):
    cut = []
    for when, kind, first, count, slot in moves:
        for expert in range(first, first + count):
            if expert > first and ring_place(store, kind, expert) > 0:
                cut[-1][3] += 1
            else:
                cut.append([when, kind, expert, 1, slot])
    return cut


def move(wide, tall, store, semaphore, place, kind, first, count, slot):
    experts = pl.ds(first, count)
    if kind == 2:
        source = tall.at[experts, pl.ds(2 * ((place >> 1) ^ slot), 2)]
    else:
        width = store.shape[-1]
        start = pl.multiple_of((place ^ (2 * kind + slot)) * width, width)
        source = wide.at[experts, :, :, pl.ds(start, width)]
    target = store.at[slot, pl.ds(ring_place(store, kind, first), count)]
    return pltpu.make_async_copy(source, target, semaphore)


def down_at(store, place, quarter, expert):
    return quarter // 2, ring_place(store, 2, expert), (quarter ^ place) & 1


def stage_kernel(ids, wide, tall, store, semaphores):
    count = store.shape[1] - SPARE
    copies = [
        move(wide, tall, store, semaphores.at[slot], ids[0], 0, 0, count, slot) for slot in range(2)
    ]
    for copy in copies:
        copy.start()
    for copy in copies:
        copy.wait()


def stage(ids, wide, tall, width):
    shape = (2, wide.shape[0] + SPARE) + wide.shape[1:-1] + (width,)
    return pl.pallas_call(
        stage_kernel,
        out_shape=pltpu.VMEM(shape, wide.dtype),
        in_specs=[IN_SMEM, IN_HBM, IN_HBM],
        out_specs=IN_VMEM,
        scratch_shapes=[pltpu.SemaphoreType.DMA((2,))],
        compiler_params=params(5),
        cost_estimate=cost(0, wide.size),
    )(ids, in_hbm(wide), in_hbm(tall))


def up_kernel(opts, ids, *refs):
    quarters, experts, total_first, finish, planned, moves = opts
    refs = list(refs)
    if planned:
        top, payloads = planned[0], [refs.pop(0) for _ in range(planned[1])]
    else:
        placing = refs.pop(0)
    normed = refs.pop(0)
    arrived = [refs.pop(0) for _ in quarters]
    total_in = refs.pop(0) if total_first is not None else None
    wide, tall, _, result, store = [refs.pop(0) for _ in range(5)]
    if planned:
        placing, high, low = [refs.pop(0) for _ in range(3)]
    gathered, rows, semaphores = refs
    blocks, slots, tokens = placing.shape
    _, places, _, hidden, width = store.shape
    capacity = slots // (places - SPARE)
    place = ids[0]
    copies = [
        move(wide, tall, store, semaphores.at[i], place, *what)
        for i, (_, *what) in enumerate(moves)
    ]
    for copy, (when, *_) in zip(copies, moves):
        if when is None:
            copy.start()
    if planned:
        write_plan(capacity, top, ids[1], payloads, placing, high, low)
    for i, quarter in enumerate(quarters):
        start = pl.multiple_of((place ^ quarter) * width, width)
        rows[0:tokens] = normed[:, pl.ds(start, width)]
        rows[tokens:] = arrived[i][...]
        for block in range(blocks):
            picked = jnp.dot(
                placing[block, experts[0] * capacity : experts[1] * capacity],
                rows[block * tokens : (block + 1) * tokens],
                preferred_element_type=jnp.float32,
            ).astype(jnp.bfloat16)
            at = slice(block * capacity, (block + 1) * capacity)
            gathered[i, :, at, :] = picked.reshape(experts[1] - experts[0], capacity, width)

    for expert in range(*experts):
        for copy, (when, *_) in zip(copies, moves):
            if when == expert:
                copy.start()
        value = total_in[expert - total_first] if total_in is not None else None
        for i, quarter in enumerate(quarters):
            part = lax.dot_general(
                gathered[i, expert - experts[0]],
                store[quarter % 2, ring_place(store, quarter // 2, expert)].reshape(2 * hidden, width),
                CONTRACT_LAST,
                preferred_element_type=jnp.float32,
            )
            value = part if value is None else value + part
        if finish:
            gate, up = value[:, :hidden], value[:, hidden:]
            value = (gate / (1.0 + jnp.exp(-gate)) * up).astype(jnp.bfloat16)
        result[expert - experts[0]] = value
    for copy in copies:
        copy.wait()


def up_step(ids, plan, normed, arrived, total, quarters, finish, experts, moves, wide, tall, store):
    _, places, _, hidden, width = store.shape
    moves = moves_of(store, moves)
    if isinstance(plan, dict):
        planned = (plan["top"], len(plan["payloads"]))
        blocks, slots, tokens = plan["shape"]
        operands = [ids] + list(plan["payloads"])
    else:
        planned = None
        blocks, slots, tokens = plan.shape
        operands = [ids, plan]
    depth = blocks * (slots // (places - SPARE))
    operands += [normed] + list(arrived)
    total_first = None
    if total is not None:
        total_first = total[1]
        operands.append(total[0])
    in_specs = [IN_SMEM] + [IN_VMEM] * (len(operands) - 1) + [IN_HBM, IN_HBM, IN_VMEM]
    operands += [in_hbm(wide), in_hbm(tall), pinned(store)]
    count = experts[1] - experts[0]
    if finish:
        shape = jax.ShapeDtypeStruct((count, depth, hidden), jnp.bfloat16)
    else:
        shape = jax.ShapeDtypeStruct((count, depth, 2 * hidden), jnp.float32)
    shapes = (shape, pltpu.VMEM(store.shape, store.dtype))
    if planned:
        shapes += (jax.ShapeDtypeStruct((blocks, slots, tokens), jnp.bfloat16),)
        shapes += (jax.ShapeDtypeStruct((blocks, tokens, slots), jnp.bfloat16),) * 2
    opts = (quarters, experts, total_first, finish, planned, moves)
    return pl.pallas_call(
        functools.partial(up_kernel, opts),
        out_shape=shapes,
        in_specs=in_specs,
        out_specs=(IN_VMEM,) * len(shapes),
        input_output_aliases={len(operands) - 1: 1},
        scratch_shapes=[
            pltpu.VMEM((len(quarters), count, depth, width), jnp.bfloat16),
            pltpu.VMEM((blocks * tokens, width), jnp.bfloat16),
            pltpu.SemaphoreType.DMA((len(moves),)),
        ],
        compiler_params=params(5),
        cost_estimate=cost(0, wide.size * len(quarters) * count // 8),
    )(*operands)


def down_kernel(groups, pieces, has_total, moves, ids, *refs):
    refs = list(refs)
    acts = [[refs.pop(0) for _ in group] for group in pieces]
    total_in = refs.pop(0) if has_total else None
    copies = []
    if moves:
        wide, tall, _, result, store, semaphores = refs
        for i, (_, *what) in enumerate(moves):
            copies.append(move(wide, tall, store, semaphores.at[i], ids[0], *what))
        for copy in copies:
            copy.start()
    else:
        store, result = refs
    for group, (low, high) in enumerate(groups):
        for expert in range(low, high):
            for copy, (when, *_) in zip(copies, moves):
                if when == expert:
                    copy.wait()
            value = total_in[expert] if has_total else None
            for act, q in zip(acts[group], pieces[group]):
                weights = store[down_at(store, ids[0], q, expert)]
                part = jnp.dot(act[expert - low], weights, preferred_element_type=jnp.float32)
                value = part if value is None else value + part
            result[expert] = value
    for copy, (when, *_) in zip(copies, moves):
        if when is None:
            copy.wait()


def down_step(ids, groups, acts, store, total, moves=(), wide=None, tall=None):
    pieces = [tuple(sorted(group)) for group in acts]
    local_experts, width = store.shape[1] - SPARE, store.shape[-1]
    moves = moves_of(store, moves)
    depth = acts[0][pieces[0][0]].shape[1]
    operands = [ids] + [group[q] for group, piece in zip(acts, pieces) for q in piece]
    in_specs = [IN_SMEM] + [IN_VMEM] * (len(operands) - 1)
    aliases, scratch = {}, []
    if total is not None:
        aliases = {len(operands): 0}
        operands.append(total)
        in_specs.append(IN_VMEM)
    shapes = (jax.ShapeDtypeStruct((local_experts, depth, width), jnp.float32),)
    if moves:
        operands += [in_hbm(wide), in_hbm(tall)]
        in_specs += [IN_HBM, IN_HBM]
        aliases[len(operands)] = 1
        shapes += (pltpu.VMEM(store.shape, store.dtype),)
        scratch = [pltpu.SemaphoreType.DMA((len(moves),))]
    operands.append(pinned(store))
    in_specs.append(IN_VMEM)
    return pl.pallas_call(
        functools.partial(down_kernel, groups, pieces, total is not None, moves),
        out_shape=shapes,
        in_specs=in_specs,
        out_specs=(IN_VMEM,) * len(shapes),
        input_output_aliases=aliases,
        scratch_shapes=scratch,
        compiler_params=params(5),
        cost_estimate=cost(0, 4 * MIB * len(acts)),
    )(*operands)


def finish_kernel(opts, ids, *refs):
    groups, quarter = opts
    refs = list(refs)
    acts = [refs.pop(0) for _ in groups]
    store, total, high, low, tokens = [refs.pop(0) for _ in range(5)]
    *results, slots_out = refs
    local_experts, depth, whole = total.shape
    blocks = high.shape[0]
    capacity = depth // blocks
    for act, group in zip(acts, groups):
        for expert in range(*group):
            weights = store[down_at(store, ids[0], quarter, expert)]
            value = jnp.dot(act[expert - group[0]], weights, preferred_element_type=jnp.float32)
            value = (value + total[expert]).astype(jnp.bfloat16)
            own = slice(expert * capacity, (expert + 1) * capacity)
            for block in range(blocks):
                slots_out[block, own, :] = value[block * capacity : (block + 1) * capacity]
    start = pl.multiple_of(ids[0] * whole, LANES)
    for block in range(blocks):
        value = jnp.dot(
            high[block], slots_out[block], preferred_element_type=jnp.float32
        ) + jnp.dot(low[block], slots_out[block], preferred_element_type=jnp.float32)
        if block == 0:
            value = value + tokens[:, pl.ds(start, whole)].astype(jnp.float32)
        results[block][...] = value.astype(jnp.bfloat16)


def finish_step(ids, groups, acts, quarter, store, total, high, low, tokens):
    blocks, count, slots = high.shape
    whole = total.shape[2]
    operands = [ids] + list(acts)
    operands += [pinned(store), total, high, low, tokens]
    shape = jax.ShapeDtypeStruct((count, whole), jnp.bfloat16)
    return pl.pallas_call(
        functools.partial(finish_kernel, (groups, quarter)),
        out_shape=(shape,) * blocks,
        in_specs=[IN_SMEM] + [IN_VMEM] * (len(operands) - 1),
        out_specs=(IN_VMEM,) * blocks,
        scratch_shapes=[pltpu.VMEM((blocks, slots, whole), jnp.bfloat16)],
        compiler_params=params(5),
        cost_estimate=cost(0, 0),
    )(*operands)


def sum_kernel(*refs):
    *parts, result = refs
    result[0] = sum(part[...].astype(jnp.float32) for part in parts).astype(jnp.bfloat16)


def gathered_tokens(activations, routes, gate_weights, norm_gain, gate_up_weights, down_weights):
    tokens = activations[0]
    token_count, features = tokens.shape
    local_experts = gate_up_weights.shape[0]
    rows = lax.axis_size("expert")
    dp_devices = lax.axis_size("dp")
    sections = lax.axis_size("section")
    capacity = token_count * routes.shape[2] // (local_experts * rows)
    slots = local_experts * capacity
    width = features // dp_devices
    ids = jnp.stack([lax.axis_index("dp"), lax.axis_index("expert") * local_experts])
    ids = ids.astype(jnp.int32)

    normed, own = normalize(ids, tokens, norm_gain, routes[0].T, gate_weights[0].T, width)
    blocks = [flipped(own, "expert", j) for j in range(1, rows)]
    wide = gate_up_weights
    tall = down_weights.reshape(local_experts, dp_devices, -1, width)
    store = stage(ids, wide, tall, width)
    mine = collect(blocks, token_count, width, store)
    across = flipped(mine, "dp", 2)
    beside = flipped(mine, "dp", 1)
    cut = local_experts - 3 * local_experts // 8
    first, second = groups = ((0, cut), (cut, local_experts))

    end = local_experts
    moves = [(None, 1, 0, 1, slot) for slot in range(2)]
    moves += [(e, 1, e - 1, 2, slot) for e in range(2, end, 2) for slot in range(2)][:-1]
    payload = {
        "payloads": [own] + blocks,
        "top": routes.shape[2],
        "shape": (rows, slots, token_count),
    }

    total, store, placing, high, low = up_step(
        ids, payload, normed, [mine, beside], None, (0, 1), False, (0, local_experts),
        moves, wide, tall, store,
    )
    across = relayed(across, total)
    far = flipped(across, "dp", 1)

    step = functools.partial(up_step, ids, placing, normed)
    moves = [(None, 1, end - 3, 2, 1), (None, 1, end - 1, 1, 0), (None, 2, 0, 1, 0)]
    partial, store = step([across], (total, 0), (2,), False, first, moves, wide, tall, store)
    moves = [(None, 1, end - 1, 1, 1), (None, 2, 1, cut - 1, 0)]
    act, store = step([far], (partial, 0), (3,), True, first, moves, wide, tall, store)
    acts = [{0: act, 1: flipped(act, "dp", 1), 2: flipped(act, "dp", 2)}]
    moves = [(None, 2, cut, 1, 0), (None, 2, 0, cut - 1, 1)]
    moves += [(e, 2, e, 1, 0) for e in range(cut + 1, end - 1)]
    act, store = step(
        [across, far], (total, 0), (2, 3), True, second, moves, wide, tall, store
    )
    acts.append({0: act, 1: flipped(act, "dp", 1), 2: flipped(act, "dp", 2)})
    near = [acts[0], {0: acts[1][0]}]
    moves = [(cut - 1, 2, cut - 1, 1, 1), (end - 1, 2, end - 1, 1, 0)]
    moves.append((None, 2, cut, end - cut, 1))
    summed, store = down_step(ids, groups, near, store, None, moves, wide, tall)
    last = relayed(acts[1][2], summed)
    far = [flipped(act, "dp", 1) for act in (acts[0][2], last)]
    pieces = [{1: acts[1][1], 2: last}]
    (summed,) = down_step(ids, (second,), pieces, store, summed)
    sums = finish_step(ids, groups, far, 3, store, summed, high, low, tokens)
    received = []
    for j in range(rows):
        route = [
            (s * rows + e, ((s + 1) % sections) * rows + (e ^ j))
            for s in range(sections)
            for e in range(rows)
        ]
        received.append(lax.ppermute(sums[j], ("section", "expert"), route))
    return pl.pallas_call(
        sum_kernel,
        out_shape=jax.ShapeDtypeStruct((1, token_count, width), jnp.bfloat16),
        in_specs=[IN_VMEM] * len(received),
        out_specs=IN_VMEM,
        compiler_params=params(5),
    )(*received)


def routed_rows(activations, routes, gate_weights, norm_gain, gate_up_weights, down_weights):
    tokens_here = activations[0]
    token_count, feature_count = tokens_here.shape
    top_count = routes.shape[2]
    local_experts = gate_up_weights.shape[0]
    expert_devices = lax.axis_size("expert")
    dp_devices = lax.axis_size("dp")
    total_experts = local_experts * expert_devices
    window = max(1, token_count * top_count // (total_experts * dp_devices))
    capacity = window * dp_devices
    slice_width = feature_count // dp_devices
    dp_place = lax.axis_index("dp")
    widened = tokens_here.astype(jnp.float32)
    mean_square = jnp.mean(widened * widened, axis=-1, keepdims=True)
    normed = (widened * lax.rsqrt(mean_square + 1e-06) * norm_gain.astype(jnp.float32)).astype(
        jnp.bfloat16
    )
    flat_routes = routes[0].reshape(-1)
    experts_iota = jnp.arange(total_experts, dtype=jnp.int32)
    onehot = (flat_routes[:, None] == experts_iota[None, :]).astype(jnp.int32)
    slot_ranks = jnp.sum((jnp.cumsum(onehot, axis=0) - onehot) * onehot, axis=1)
    targets = flat_routes * capacity + slot_ranks
    contract_rows = (((0,), (0,)), ((), ()))
    slot_iota = jnp.arange(total_experts * capacity, dtype=jnp.int32)
    matches = (targets[:, None] == slot_iota[None, :]).reshape(
        token_count, top_count, total_experts * capacity
    )
    placing = jnp.any(matches, axis=1).astype(jnp.bfloat16)
    normed_slice = lax.dynamic_slice_in_dim(normed, dp_place * slice_width, slice_width, 1)
    outgoing = lax.dot_general(
        placing, normed_slice, contract_rows, preferred_element_type=jnp.float32
    )
    outgoing = outgoing.astype(jnp.bfloat16).reshape(total_experts, capacity, slice_width)
    arriving = lax.all_to_all(outgoing, "expert", split_axis=0, concat_axis=0, tiled=True)
    arriving = arriving.reshape(expert_devices, local_experts, capacity, slice_width)
    weights_part = gate_up_weights
    gate_up = jnp.einsum(
        "seck,ejhk->jsech",
        lax.all_gather(arriving, "dp", axis=3, tiled=True),
        weights_part,
        preferred_element_type=jnp.float32,
    )
    hidden_act = (jax.nn.silu(gate_up[0]) * gate_up[1]).astype(jnp.bfloat16)
    weights_part = down_weights
    summed = jnp.einsum(
        "sech,ehf->secf",
        lax.all_gather(hidden_act, "dp", axis=3, tiled=True),
        weights_part,
        preferred_element_type=jnp.float32,
    )
    expert_out = summed.astype(jnp.bfloat16)
    returned = lax.all_to_all(expert_out, "expert", split_axis=0, concat_axis=0, tiled=True)
    returned_flat = returned.reshape(total_experts * capacity, slice_width)
    picked = jnp.take(returned_flat, targets, axis=0).reshape(token_count, top_count, slice_width)
    branch = jnp.sum(picked.astype(jnp.float32) * gate_weights[0][:, :, None], axis=1)
    residual = lax.dynamic_slice_in_dim(widened, dp_place * slice_width, slice_width, 1)
    finished = (residual + branch).astype(jnp.bfloat16)
    arrived = shifted(finished, "section", 1)
    return arrived[None]


def body(activations, routes, gate_weights, norm_gain, gate_up_weights, down_weights):
    token_count, top_count = routes.shape[1], routes.shape[2]
    local_experts = gate_up_weights.shape[0]
    rows = lax.axis_size("expert")
    capacity = token_count * top_count // (local_experts * rows)
    few = token_count <= local_experts * capacity and local_experts % 8 == 0
    aligned = capacity % 16 == 0 and token_count % 16 == 0
    suits = rows == 4 and lax.axis_size("dp") == 4 and token_count * 2 == LANES
    form = gathered_tokens if few and aligned and suits else routed_rows
    return form(
        activations, routes, gate_weights, norm_gain, gate_up_weights, down_weights
    )


def solution(mesh):
    placed = (
        P("section", "expert", None),
        P("section", "expert", None),
        P("section", "expert", None),
        P(),
        P("expert", None, "dp", None),
        P("expert", None, "dp"),
    )
    return jax.shard_map(
        body, mesh=mesh, in_specs=placed, out_specs=P("section", "expert", "dp"), check_vma=False
    )
```

```python
import functools

import jax
import jax.numpy as jnp
from jax import lax
from jax.experimental import pallas as pl
from jax.experimental.pallas import tpu as pltpu
from jax.sharding import PartitionSpec as P

CONTRACT_LAST = (((1,), (1,)), ((), ()))
IN_VMEM = pl.BlockSpec(memory_space=pltpu.VMEM)
IN_SMEM = pl.BlockSpec(memory_space=pltpu.SMEM)
IN_HBM = pl.BlockSpec(memory_space=pltpu.HBM)
MIB = 1 << 20
LANES = 128
SPARE = 1


def params(mib):
    return pltpu.CompilerParams(vmem_limit_bytes=mib * MIB)


def cost(flops, moved):
    return pl.CostEstimate(flops=int(flops), bytes_accessed=int(moved), transcendentals=0)


def pinned(array):
    return pltpu.with_memory_space_constraint(array, pltpu.VMEM)


def in_hbm(array):
    return pltpu.with_memory_space_constraint(array, pltpu.HBM)


def shifted(block, axis, distance):
    count = lax.axis_size(axis)
    return lax.ppermute(block, axis, [((i - distance) % count, i) for i in range(count)])


def flipped(block, axis, bit):
    return lax.ppermute(block, axis, [(i, i ^ bit) for i in range(lax.axis_size(axis))])


def norm_kernel(ids, *refs):
    sources, (normed, sent), landed, semaphores = refs[:4], refs[4:6], refs[6:10], refs[10]
    copies = [
        pltpu.make_async_copy(source, target, semaphores.at[i])
        for i, (source, target) in enumerate(zip(sources, landed))
    ]
    for copy in copies:
        copy.start()
    for copy in copies:
        copy.wait()
    tokens, gain, routes, weights = landed
    widened = tokens[...].astype(jnp.float32)
    mean_square = jnp.mean(widened * widened, axis=-1, keepdims=True)
    rows = widened * lax.rsqrt(mean_square + 1e-06)
    rows = rows * gain[...].astype(jnp.float32).reshape(1, rows.shape[1])
    normed[...] = rows.astype(jnp.bfloat16)
    count, features = normed.shape
    pieces = sent.shape[0] // count
    start = pl.multiple_of(ids[0] * pieces * LANES, pieces * LANES)
    for i in range(pieces):
        at = pl.ds(pl.multiple_of(start + i * LANES, LANES), LANES)
        sent[i * count : (i + 1) * count] = normed[:, at]
    whole = weights[...]
    coarse = whole.astype(jnp.bfloat16).astype(jnp.float32)
    middle = (whole - coarse).astype(jnp.bfloat16).astype(jnp.float32)
    fine = whole - coarse - middle
    upper = jnp.concatenate([routes[...].astype(jnp.float32), coarse])
    lower = jnp.concatenate([middle, fine])
    sent[pieces * count :] = jnp.concatenate([upper, lower], axis=1).astype(jnp.bfloat16)


def normalize(ids, tokens, gain, routes, weights, width):
    count, features = tokens.shape
    top = routes.shape[0]
    operands = (tokens, gain, routes, weights)
    return pl.pallas_call(
        norm_kernel,
        out_shape=(
            jax.ShapeDtypeStruct((count, features), jnp.bfloat16),
            jax.ShapeDtypeStruct((count * width // LANES + 2 * top, LANES), jnp.bfloat16),
        ),
        in_specs=[IN_SMEM] + [IN_HBM] * 4,
        out_specs=(IN_VMEM, IN_VMEM),
        scratch_shapes=[pltpu.VMEM(x.shape, x.dtype) for x in operands]
        + [pltpu.SemaphoreType.DMA((4,))],
        compiler_params=params(5),
    )(ids, *(in_hbm(x) for x in operands))


def relay_kernel(block, after, result):
    result[...] = block[...]


def relayed(block, after):
    return pl.pallas_call(
        relay_kernel,
        out_shape=jax.ShapeDtypeStruct(block.shape, block.dtype),
        in_specs=[IN_VMEM, IN_VMEM],
        out_specs=IN_VMEM,
        compiler_params=params(5),
        cost_estimate=cost(0, MIB),
    )(block, after)


def collect_kernel(*refs):
    *blocks, staged, result = refs
    count = result.shape[0] // len(blocks)
    for i, block in enumerate(blocks):
        for j in range(result.shape[1] // LANES):
            result[i * count : (i + 1) * count, j * LANES : (j + 1) * LANES] = block[
                j * count : (j + 1) * count
            ]


def collect(blocks, count, width, staged):
    return pl.pallas_call(
        collect_kernel,
        out_shape=jax.ShapeDtypeStruct((len(blocks) * count, width), jnp.bfloat16),
        in_specs=[IN_VMEM] * (len(blocks) + 1),
        out_specs=IN_VMEM,
        compiler_params=params(5),
    )(*blocks, pinned(staged))


def write_plan(capacity, top, first_expert, blocks, placing, high, low):
    tokens, slots = high.shape[1:]
    count = len(blocks) * tokens
    lane = lax.broadcasted_iota(jnp.int32, (count, slots), 1)
    expert = (first_expert + lane // capacity).astype(jnp.float32)
    rank_of_lane = (lane % capacity).astype(jnp.float32)
    row = lax.broadcasted_iota(jnp.int32, (tokens, tokens), 0)
    column = lax.broadcasted_iota(jnp.int32, (tokens, tokens), 1)
    earlier = jnp.where(column < row, 1.0, 0.0).astype(jnp.bfloat16)
    sent = [block[block.shape[0] - 2 * top :].astype(jnp.float32) for block in blocks]
    upper = jnp.concatenate([part[:, :tokens] for part in sent], axis=1)
    lower = jnp.concatenate([part[:, LANES // 2 : LANES // 2 + tokens] for part in sent], axis=1)
    names = upper[:top]
    values = upper[top:] + lower[:top] + lower[top:]
    rest = jnp.zeros((LANES - 2 * top, count), jnp.float32)
    table = jnp.concatenate([names, values, rest]).T
    weight = jnp.zeros((count, slots), jnp.float32)
    named = jnp.zeros((count, slots), jnp.float32)
    for k in range(top):
        hit = table[:, k : k + 1] == expert
        weight = jnp.where(hit, table[:, top + k : top + k + 1], weight)
        named = jnp.where(hit, 1.0, named)
    for i in range(len(blocks)):
        own = slice(i * tokens, (i + 1) * tokens)
        ranks = jnp.dot(earlier, named[own].astype(jnp.bfloat16), preferred_element_type=jnp.float32)
        fits = (named[own] > 0) & (ranks == rank_of_lane[own])
        placing[i] = jnp.where(fits, 1.0, 0.0).T.astype(jnp.bfloat16)
        scaled = jnp.where(fits, weight[own], 0.0)
        coarse = scaled.astype(jnp.bfloat16)
        high[i] = coarse
        low[i] = (scaled - coarse.astype(jnp.float32)).astype(jnp.bfloat16)


def ring_place(store, kind, expert):
    _, places, _, _, _ = store.shape
    local_experts = places - SPARE
    return (kind * local_experts + expert) % places


def moves_of(store, moves):
    cut = []
    for when, kind, first, count, slot in moves:
        for expert in range(first, first + count):
            if expert > first and ring_place(store, kind, expert) > 0:
                cut[-1][3] += 1
            else:
                cut.append([when, kind, expert, 1, slot])
    return cut


def move(wide, tall, store, semaphore, place, kind, first, count, slot):
    experts = pl.ds(first, count)
    if kind == 2:
        source = tall.at[experts, pl.ds(2 * ((place >> 1) ^ slot), 2)]
    else:
        width = store.shape[-1]
        start = pl.multiple_of((place ^ (2 * kind + slot)) * width, width)
        source = wide.at[experts, :, :, pl.ds(start, width)]
    target = store.at[slot, pl.ds(ring_place(store, kind, first), count)]
    return pltpu.make_async_copy(source, target, semaphore)


def down_at(store, place, quarter, expert):
    return quarter // 2, ring_place(store, 2, expert), (quarter ^ place) & 1


def stage_kernel(ids, wide, tall, store, semaphores):
    count = store.shape[1] - SPARE
    copies = [
        move(wide, tall, store, semaphores.at[slot], ids[0], 0, 0, count, slot) for slot in range(2)
    ]
    for copy in copies:
        copy.start()
    for copy in copies:
        copy.wait()


def stage(ids, wide, tall, width):
    shape = (2, wide.shape[0] + SPARE) + wide.shape[1:-1] + (width,)
    return pl.pallas_call(
        stage_kernel,
        out_shape=pltpu.VMEM(shape, wide.dtype),
        in_specs=[IN_SMEM, IN_HBM, IN_HBM],
        out_specs=IN_VMEM,
        scratch_shapes=[pltpu.SemaphoreType.DMA((2,))],
        compiler_params=params(5),
        cost_estimate=cost(0, wide.size),
    )(ids, in_hbm(wide), in_hbm(tall))


def up_kernel(opts, ids, *refs):
    quarters, experts, total_first, finish, planned, moves = opts
    refs = list(refs)
    if planned:
        top, payloads = planned[0], [refs.pop(0) for _ in range(planned[1])]
    else:
        placing = refs.pop(0)
    normed = refs.pop(0)
    arrived = [refs.pop(0) for _ in quarters]
    total_in = refs.pop(0) if total_first is not None else None
    wide, tall, _, result, store = [refs.pop(0) for _ in range(5)]
    if planned:
        placing, high, low = [refs.pop(0) for _ in range(3)]
    gathered, rows, semaphores = refs
    blocks, slots, tokens = placing.shape
    _, places, _, hidden, width = store.shape
    capacity = slots // (places - SPARE)
    place = ids[0]
    copies = [
        move(wide, tall, store, semaphores.at[i], place, *what)
        for i, (_, *what) in enumerate(moves)
    ]
    for copy, (when, *_) in zip(copies, moves):
        if when is None:
            copy.start()
    if planned:
        write_plan(capacity, top, ids[1], payloads, placing, high, low)
    for i, quarter in enumerate(quarters):
        start = pl.multiple_of((place ^ quarter) * width, width)
        rows[0:tokens] = normed[:, pl.ds(start, width)]
        rows[tokens:] = arrived[i][...]
        for block in range(blocks):
            picked = jnp.dot(
                placing[block, experts[0] * capacity : experts[1] * capacity],
                rows[block * tokens : (block + 1) * tokens],
                preferred_element_type=jnp.float32,
            ).astype(jnp.bfloat16)
            at = slice(block * capacity, (block + 1) * capacity)
            gathered[i, :, at, :] = picked.reshape(experts[1] - experts[0], capacity, width)

    for expert in range(*experts):
        for copy, (when, *_) in zip(copies, moves):
            if when == expert:
                copy.start()
        value = total_in[expert - total_first] if total_in is not None else None
        for i, quarter in enumerate(quarters):
            part = lax.dot_general(
                gathered[i, expert - experts[0]],
                store[quarter % 2, ring_place(store, quarter // 2, expert)].reshape(2 * hidden, width),
                CONTRACT_LAST,
                preferred_element_type=jnp.float32,
            )
            value = part if value is None else value + part
        if finish:
            gate, up = value[:, :hidden], value[:, hidden:]
            value = (gate / (1.0 + jnp.exp(-gate)) * up).astype(jnp.bfloat16)
        result[expert - experts[0]] = value
    for copy in copies:
        copy.wait()


def up_step(ids, plan, normed, arrived, total, quarters, finish, experts, moves, wide, tall, store):
    _, places, _, hidden, width = store.shape
    moves = moves_of(store, moves)
    if isinstance(plan, dict):
        planned = (plan["top"], len(plan["payloads"]))
        blocks, slots, tokens = plan["shape"]
        operands = [ids] + list(plan["payloads"])
    else:
        planned = None
        blocks, slots, tokens = plan.shape
        operands = [ids, plan]
    depth = blocks * (slots // (places - SPARE))
    operands += [normed] + list(arrived)
    total_first = None
    if total is not None:
        total_first = total[1]
        operands.append(total[0])
    in_specs = [IN_SMEM] + [IN_VMEM] * (len(operands) - 1) + [IN_HBM, IN_HBM, IN_VMEM]
    operands += [in_hbm(wide), in_hbm(tall), pinned(store)]
    count = experts[1] - experts[0]
    if finish:
        shape = jax.ShapeDtypeStruct((count, depth, hidden), jnp.bfloat16)
    else:
        shape = jax.ShapeDtypeStruct((count, depth, 2 * hidden), jnp.float32)
    shapes = (shape, pltpu.VMEM(store.shape, store.dtype))
    if planned:
        shapes += (jax.ShapeDtypeStruct((blocks, slots, tokens), jnp.bfloat16),)
        shapes += (jax.ShapeDtypeStruct((blocks, tokens, slots), jnp.bfloat16),) * 2
    opts = (quarters, experts, total_first, finish, planned, moves)
    return pl.pallas_call(
        functools.partial(up_kernel, opts),
        out_shape=shapes,
        in_specs=in_specs,
        out_specs=(IN_VMEM,) * len(shapes),
        input_output_aliases={len(operands) - 1: 1},
        scratch_shapes=[
            pltpu.VMEM((len(quarters), count, depth, width), jnp.bfloat16),
            pltpu.VMEM((blocks * tokens, width), jnp.bfloat16),
            pltpu.SemaphoreType.DMA((len(moves),)),
        ],
        compiler_params=params(5),
        cost_estimate=cost(0, wide.size * len(quarters) * count // 8),
    )(*operands)


def down_kernel(groups, pieces, has_total, moves, ids, *refs):
    refs = list(refs)
    acts = [[refs.pop(0) for _ in group] for group in pieces]
    total_in = refs.pop(0) if has_total else None
    copies = []
    if moves:
        wide, tall, _, result, store, semaphores = refs
        for i, (_, *what) in enumerate(moves):
            copies.append(move(wide, tall, store, semaphores.at[i], ids[0], *what))
        for copy in copies:
            copy.start()
    else:
        store, result = refs
    for group, (low, high) in enumerate(groups):
        for expert in range(low, high):
            for copy, (when, *_) in zip(copies, moves):
                if when == expert:
                    copy.wait()
            value = total_in[expert] if has_total else None
            for act, q in zip(acts[group], pieces[group]):
                weights = store[down_at(store, ids[0], q, expert)]
                part = jnp.dot(act[expert - low], weights, preferred_element_type=jnp.float32)
                value = part if value is None else value + part
            result[expert] = value
    for copy, (when, *_) in zip(copies, moves):
        if when is None:
            copy.wait()


def down_step(ids, groups, acts, store, total, moves=(), wide=None, tall=None):
    pieces = [tuple(sorted(group)) for group in acts]
    local_experts, width = store.shape[1] - SPARE, store.shape[-1]
    moves = moves_of(store, moves)
    depth = acts[0][pieces[0][0]].shape[1]
    operands = [ids] + [group[q] for group, piece in zip(acts, pieces) for q in piece]
    in_specs = [IN_SMEM] + [IN_VMEM] * (len(operands) - 1)
    aliases, scratch = {}, []
    if total is not None:
        aliases = {len(operands): 0}
        operands.append(total)
        in_specs.append(IN_VMEM)
    shapes = (jax.ShapeDtypeStruct((local_experts, depth, width), jnp.float32),)
    if moves:
        operands += [in_hbm(wide), in_hbm(tall)]
        in_specs += [IN_HBM, IN_HBM]
        aliases[len(operands)] = 1
        shapes += (pltpu.VMEM(store.shape, store.dtype),)
        scratch = [pltpu.SemaphoreType.DMA((len(moves),))]
    operands.append(pinned(store))
    in_specs.append(IN_VMEM)
    return pl.pallas_call(
        functools.partial(down_kernel, groups, pieces, total is not None, moves),
        out_shape=shapes,
        in_specs=in_specs,
        out_specs=(IN_VMEM,) * len(shapes),
        input_output_aliases=aliases,
        scratch_shapes=scratch,
        compiler_params=params(5),
        cost_estimate=cost(0, 4 * MIB * len(acts)),
    )(*operands)


def finish_kernel(opts, ids, *refs):
    groups, quarter = opts
    refs = list(refs)
    acts = [refs.pop(0) for _ in groups]
    store, total, high, low, tokens = [refs.pop(0) for _ in range(5)]
    *results, slots_out = refs
    local_experts, depth, whole = total.shape
    blocks = high.shape[0]
    capacity = depth // blocks
    for act, group in zip(acts, groups):
        for expert in range(*group):
            weights = store[down_at(store, ids[0], quarter, expert)]
            value = jnp.dot(act[expert - group[0]], weights, preferred_element_type=jnp.float32)
            value = (value + total[expert]).astype(jnp.bfloat16)
            own = slice(expert * capacity, (expert + 1) * capacity)
            for block in range(blocks):
                slots_out[block, own, :] = value[block * capacity : (block + 1) * capacity]
    start = pl.multiple_of(ids[0] * whole, LANES)
    for block in range(blocks):
        value = jnp.dot(
            high[block], slots_out[block], preferred_element_type=jnp.float32
        ) + jnp.dot(low[block], slots_out[block], preferred_element_type=jnp.float32)
        if block == 0:
            value = value + tokens[:, pl.ds(start, whole)].astype(jnp.float32)
        results[block][...] = value.astype(jnp.bfloat16)


def finish_step(ids, groups, acts, quarter, store, total, high, low, tokens):
    blocks, count, slots = high.shape
    whole = total.shape[2]
    operands = [ids] + list(acts)
    operands += [pinned(store), total, high, low, tokens]
    shape = jax.ShapeDtypeStruct((count, whole), jnp.bfloat16)
    return pl.pallas_call(
        functools.partial(finish_kernel, (groups, quarter)),
        out_shape=(shape,) * blocks,
        in_specs=[IN_SMEM] + [IN_VMEM] * (len(operands) - 1),
        out_specs=(IN_VMEM,) * blocks,
        scratch_shapes=[pltpu.VMEM((blocks, slots, whole), jnp.bfloat16)],
        compiler_params=params(5),
        cost_estimate=cost(0, 0),
    )(*operands)


def sum_kernel(*refs):
    *parts, result = refs
    result[0] = sum(part[...].astype(jnp.float32) for part in parts).astype(jnp.bfloat16)


def gathered_tokens(activations, routes, gate_weights, norm_gain, gate_up_weights, down_weights):
    tokens = activations[0]
    token_count, features = tokens.shape
    local_experts = gate_up_weights.shape[0]
    rows = lax.axis_size("expert")
    dp_devices = lax.axis_size("dp")
    sections = lax.axis_size("section")
    capacity = token_count * routes.shape[2] // (local_experts * rows)
    slots = local_experts * capacity
    width = features // dp_devices
    ids = jnp.stack([lax.axis_index("dp"), lax.axis_index("expert") * local_experts])
    ids = ids.astype(jnp.int32)

    normed, own = normalize(ids, tokens, norm_gain, routes[0].T, gate_weights[0].T, width)
    blocks = [flipped(own, "expert", j) for j in range(1, rows)]
    wide = gate_up_weights
    tall = down_weights.reshape(local_experts, dp_devices, -1, width)
    store = stage(ids, wide, tall, width)
    mine = collect(blocks, token_count, width, store)
    across = flipped(mine, "dp", 2)
    beside = flipped(mine, "dp", 1)
    cut = local_experts - 3 * local_experts // 8
    first, second = groups = ((0, cut), (cut, local_experts))

    end = local_experts
    moves = [(None, 1, 0, 1, slot) for slot in range(2)]
    moves += [(e, 1, e - 1, 2, slot) for e in range(2, end, 2) for slot in range(2)][:-1]
    payload = {
        "payloads": [own] + blocks,
        "top": routes.shape[2],
        "shape": (rows, slots, token_count),
    }

    total, store, placing, high, low = up_step(
        ids, payload, normed, [mine, beside], None, (0, 1), False, (0, local_experts),
        moves, wide, tall, store,
    )
    across = relayed(across, total)
    far = flipped(across, "dp", 1)

    step = functools.partial(up_step, ids, placing, normed)
    moves = [(None, 1, end - 3, 2, 1), (None, 1, end - 1, 1, 0), (None, 2, 0, 1, 0)]
    partial, store = step([across], (total, 0), (2,), False, first, moves, wide, tall, store)
    moves = [(None, 1, end - 1, 1, 1), (None, 2, 1, cut - 1, 0)]
    act, store = step([far], (partial, 0), (3,), True, first, moves, wide, tall, store)
    acts = [{0: act, 1: flipped(act, "dp", 1), 2: flipped(act, "dp", 2)}]
    moves = [(None, 2, cut, 1, 0), (None, 2, 0, cut - 1, 1)]
    moves += [(e, 2, e, 1, 0) for e in range(cut + 1, end - 1)]
    act, store = step(
        [across, far], (total, 0), (2, 3), True, second, moves, wide, tall, store
    )
    acts.append({0: act, 1: flipped(act, "dp", 1), 2: flipped(act, "dp", 2)})
    near = [acts[0], {0: acts[1][0]}]
    moves = [(cut - 1, 2, cut - 1, 1, 1), (end - 1, 2, end - 1, 1, 0)]
    moves.append((None, 2, cut, end - cut, 1))
    summed, store = down_step(ids, groups, near, store, None, moves, wide, tall)
    last = relayed(acts[1][2], summed)
    far = [flipped(act, "dp", 1) for act in (acts[0][2], last)]
    pieces = [{1: acts[1][1], 2: last}]
    (summed,) = down_step(ids, (second,), pieces, store, summed)
    sums = finish_step(ids, groups, far, 3, store, summed, high, low, tokens)
    received = []
    for j in range(rows):
        route = [
            (s * rows + e, ((s + 1) % sections) * rows + (e ^ j))
            for s in range(sections)
            for e in range(rows)
        ]
        received.append(lax.ppermute(sums[j], ("section", "expert"), route))
    return pl.pallas_call(
        sum_kernel,
        out_shape=jax.ShapeDtypeStruct((1, token_count, width), jnp.bfloat16),
        in_specs=[IN_VMEM] * len(received),
        out_specs=IN_VMEM,
        compiler_params=params(5),
    )(*received)


def routed_rows(activations, routes, gate_weights, norm_gain, gate_up_weights, down_weights):
    tokens_here = activations[0]
    token_count, feature_count = tokens_here.shape
    top_count = routes.shape[2]
    local_experts = gate_up_weights.shape[0]
    expert_devices = lax.axis_size("expert")
    dp_devices = lax.axis_size("dp")
    total_experts = local_experts * expert_devices
    window = max(1, token_count * top_count // (total_experts * dp_devices))
    capacity = window * dp_devices
    slice_width = feature_count // dp_devices
    dp_place = lax.axis_index("dp")
    widened = tokens_here.astype(jnp.float32)
    mean_square = jnp.mean(widened * widened, axis=-1, keepdims=True)
    normed = (widened * lax.rsqrt(mean_square + 1e-06) * norm_gain.astype(jnp.float32)).astype(
        jnp.bfloat16
    )
    flat_routes = routes[0].reshape(-1)
    experts_iota = jnp.arange(total_experts, dtype=jnp.int32)
    onehot = (flat_routes[:, None] == experts_iota[None, :]).astype(jnp.int32)
    slot_ranks = jnp.sum((jnp.cumsum(onehot, axis=0) - onehot) * onehot, axis=1)
    targets = flat_routes * capacity + slot_ranks
    contract_rows = (((0,), (0,)), ((), ()))
    slot_iota = jnp.arange(total_experts * capacity, dtype=jnp.int32)
    matches = (targets[:, None] == slot_iota[None, :]).reshape(
        token_count, top_count, total_experts * capacity
    )
    placing = jnp.any(matches, axis=1).astype(jnp.bfloat16)
    normed_slice = lax.dynamic_slice_in_dim(normed, dp_place * slice_width, slice_width, 1)
    outgoing = lax.dot_general(
        placing, normed_slice, contract_rows, preferred_element_type=jnp.float32
    )
    outgoing = outgoing.astype(jnp.bfloat16).reshape(total_experts, capacity, slice_width)
    arriving = lax.all_to_all(outgoing, "expert", split_axis=0, concat_axis=0, tiled=True)
    arriving = arriving.reshape(expert_devices, local_experts, capacity, slice_width)
    weights_part = gate_up_weights
    gate_up = jnp.einsum(
        "seck,ejhk->jsech",
        lax.all_gather(arriving, "dp", axis=3, tiled=True),
        weights_part,
        preferred_element_type=jnp.float32,
    )
    hidden_act = (jax.nn.silu(gate_up[0]) * gate_up[1]).astype(jnp.bfloat16)
    weights_part = down_weights
    summed = jnp.einsum(
        "sech,ehf->secf",
        lax.all_gather(hidden_act, "dp", axis=3, tiled=True),
        weights_part,
        preferred_element_type=jnp.float32,
    )
    expert_out = summed.astype(jnp.bfloat16)
    returned = lax.all_to_all(expert_out, "expert", split_axis=0, concat_axis=0, tiled=True)
    returned_flat = returned.reshape(total_experts * capacity, slice_width)
    picked = jnp.take(returned_flat, targets, axis=0).reshape(token_count, top_count, slice_width)
    branch = jnp.sum(picked.astype(jnp.float32) * gate_weights[0][:, :, None], axis=1)
    residual = lax.dynamic_slice_in_dim(widened, dp_place * slice_width, slice_width, 1)
    finished = (residual + branch).astype(jnp.bfloat16)
    arrived = shifted(finished, "section", 1)
    return arrived[None]


def body(activations, routes, gate_weights, norm_gain, gate_up_weights, down_weights):
    token_count, top_count = routes.shape[1], routes.shape[2]
    local_experts = gate_up_weights.shape[0]
    rows = lax.axis_size("expert")
    capacity = token_count * top_count // (local_experts * rows)
    few = token_count <= local_experts * capacity and local_experts % 8 == 0
    aligned = capacity % 16 == 0 and token_count % 16 == 0
    suits = rows == 4 and lax.axis_size("dp") == 4 and token_count * 2 == LANES
    form = gathered_tokens if few and aligned and suits else routed_rows
    return form(
        activations, routes, gate_weights, norm_gain, gate_up_weights, down_weights
    )


def solution(mesh):
    placed = (
        P("section", "expert", None),
        P("section", "expert", None),
        P("section", "expert", None),
        P(),
        P("expert", None, "dp", None),
        P("expert", None, "dp"),
    )
    return jax.shard_map(
        body, mesh=mesh, in_specs=placed, out_specs=P("section", "expert", "dp"), check_vma=False
    )
```
